256 devices in a mesh: section: 16 (over y_hi, x, core), mp: 16 (over y_lo, z).
Axes of the slice: x: 4, y: 4 (y_hi: 2, y_lo: 2; y = y_hi * 2 + y_lo), z: 8, core: 2. Of those that a mesh axis runs over, the one named last changes fastest.
Arguments:
- tokens: bfloat16 [512, 8192], P('mp', 'section'), may hold values from -18 to 18
- upstream: bfloat16 [512, 8192], P('mp', 'section'), may hold values from -6 to 6
- norm_gain: bfloat16 [8192], P('section'), may hold values from 0.25 to 1.75
- gate_weight: bfloat16 [8192, 28672], P('section', 'mp'), may hold values from -0.0625 to 0.0625
- up_weight: bfloat16 [8192, 28672], P('section', 'mp'), may hold values from -0.0625 to 0.0625
- down_weight: bfloat16 [28672, 8192], P('mp', 'section'), may hold values from -0.03125 to 0.03125
- gate_mask: int32 [128, 448], P('section', 'mp'), may hold values 0 or 1
- up_mask: int32 [128, 448], P('section', 'mp'), may hold values 0 or 1
- down_mask: int32 [448, 128], P('mp', 'section'), may hold values 0 or 1
Outputs:
- layer_out: bfloat16 [512, 8192], P('mp', 'section')
- input_grad: bfloat16 [512, 8192], P('mp', 'section')
- gate_grad: bfloat16 [8192, 28672], P('section', 'mp')
- up_grad: bfloat16 [8192, 28672], P('section', 'mp')
- down_grad: bfloat16 [28672, 8192], P('mp', 'section')
The draws below stay inside these ranges and needn't reach their ends.
Inputs may be any that keep to these rules, and one draw needn't show every extreme that they name: `gate_mask`: 1 keeps the 64 x 64 block of the gate projection, 0 removes it. `up_mask`: 1 keeps the 64 x 64 block of the up projection, 0 removes it. `down_mask`: 1 keeps the 64 x 64 block of the down projection, 0 removes it.
All inputs are finite; a program needn't handle non-finite values.
Results may differ from the reference program's by a relative error of at most 0.02.
Values may be sent and summed in bfloat16 or wider, within the bound.
A program may use at most 128 MiB of HBM per device.

```python
import jax
import jax.numpy as jnp
from jax import lax

D = 8192
FF = 28672
BLOCK = 64
TOKENS = 512
N_SECTION = 16
N_MP = 16


def draw_tokens(key, part):
    key = jax.random.fold_in(key, 11)
    position = jnp.arange(D, dtype=jnp.float32) / (D - 1)
    column_scale = 0.6 * jnp.exp(position * jnp.log(4.0))
    values = jax.random.truncated_normal(key, -6.0, 6.0, (TOKENS, D), jnp.float32)
    return (values * column_scale[None, :]).astype(jnp.bfloat16)


def with_ends(drawn, key, least, high):
    index_at = [jax.random.randint(jax.random.fold_in(key, axis), (), 0, length) for axis, length in enumerate(drawn.shape)]
    main_axis = drawn.shape.index(max(drawn.shape))
    neighbour = index_at[:main_axis] + [(index_at[main_axis] + 1) % drawn.shape[main_axis]] + index_at[main_axis + 1:]
    return drawn.at[tuple(index_at)].set(least).at[tuple(neighbour)].set(high)


def level_of(stream_key, extent, pieces, low, largest):
    gain, own = 1.0, jax.random.fold_in(stream_key, 6)
    for dim, blocks in pieces:
        steps = jnp.exp(jax.random.uniform(jax.random.fold_in(own, dim), (blocks,), jnp.float32, low / len(pieces), largest / len(pieces)))
        gain = gain * jnp.repeat(steps, extent[dim] // blocks).reshape([-1 if axis == dim else 1 for axis in range(len(extent))])
    return gain


def centred(rng, dims, scale, most, split=(), kind=jnp.bfloat16):
    loudness = level_of(rng, dims, split, -0.22, 0.18) if split else 1.0
    entries = jax.random.normal(rng, dims, jnp.float32) * scale * loudness
    return jnp.minimum(jnp.maximum(entries, -most), most).astype(kind)


def setup_inputs(seed: int = 0) -> dict:
    seeds = jax.random.split(jax.random.key(seed), 10)
    return {
        "tokens": draw_tokens(jax.random.fold_in(seeds[9], 71), 0),
        "upstream": centred(seeds[1], (TOKENS, D), 1.0, 6.0, ((0, 16), (1, 16))),
        "norm_gain": jnp.clip(1.0 + 0.15 * jax.random.normal(seeds[2], (D,), jnp.float32), 0.25, 1.75).astype(jnp.bfloat16),
        "gate_weight": centred(seeds[3], (D, FF), D ** -0.5, 0.0625, ((0, 16), (1, 16))),
        "up_weight": centred(seeds[4], (D, FF), D ** -0.5, 0.0625, ((0, 16), (1, 16))),
        "down_weight": centred(seeds[5], (FF, D), FF ** -0.5, 0.03125, ((0, 16), (1, 16))),
        "gate_mask": with_ends((jax.random.randint(seeds[6], (D // BLOCK, FF // BLOCK), 0, 2) < 1).astype(jnp.int32), jax.random.fold_in(seeds[6], 1), 0, 1),
        "up_mask": with_ends((jax.random.randint(seeds[7], (D // BLOCK, FF // BLOCK), 0, 2) < 1).astype(jnp.int32), jax.random.fold_in(seeds[7], 1), 0, 1),
        "down_mask": with_ends((jax.random.randint(seeds[8], (FF // BLOCK, D // BLOCK), 0, 2) < 1).astype(jnp.int32), jax.random.fold_in(seeds[8], 1), 0, 1),
    }


EPSILON = 1e-05

def expand(marks):
    rows_count, cols_count = marks.shape
    widened = marks.astype(jnp.bfloat16)
    return jnp.broadcast_to(widened[:, None, :, None], (rows_count, BLOCK, cols_count, BLOCK)).reshape(rows_count * BLOCK, cols_count * BLOCK)

def blocked(operand_pairs, blocks_count, contract_dim):
    first_left, first_right = operand_pairs[0]
    span = first_left.shape[1] // blocks_count
    row_count = first_left.shape[0]
    col_count = first_right.shape[1 - contract_dim]

    def advance(running, position):
        partial_value = jnp.zeros((row_count, col_count), jnp.float32)
        for left_side, right_side in operand_pairs:
            left_piece = lax.dynamic_slice_in_dim(left_side, position * span, span, 1)
            right_piece = lax.dynamic_slice_in_dim(right_side, position * span, span, contract_dim)
            partial_value = partial_value + lax.dot_general(left_piece, right_piece, (((1,), (contract_dim,)), ((), ())), preferred_element_type=jnp.float32)
        rounded = lax.optimization_barrier(partial_value.astype(jnp.bfloat16))
        return (running + rounded.astype(jnp.float32), None)
    running, _ = lax.scan(advance, jnp.zeros((row_count, col_count), jnp.float32), jnp.arange(blocks_count, dtype=jnp.int32))
    return running

def reference(tokens, upstream, norm_gain, gate_weight, up_weight, down_weight, gate_mask, up_mask, down_mask):
    inputs_f = tokens.astype(jnp.float32)
    inv_rms = lax.rsqrt(lax.optimization_barrier(jnp.mean(inputs_f * inputs_f, axis=1, keepdims=True)) + EPSILON)
    scaled = inputs_f * inv_rms
    gain_f = norm_gain.astype(jnp.float32)
    normed = (scaled * gain_f).astype(jnp.bfloat16)
    gate_eff = gate_weight * expand(gate_mask)
    up_eff = up_weight * expand(up_mask)
    down_eff = down_weight * expand(down_mask)
    gate_pre = blocked(((normed, gate_eff),), N_SECTION, 0)
    up_pre = blocked(((normed, up_eff),), N_SECTION, 0)
    sigmoid_gate = jax.nn.sigmoid(gate_pre)
    activation = (gate_pre * sigmoid_gate * up_pre).astype(jnp.bfloat16)
    layer_out = (inputs_f + blocked(((activation, down_eff),), N_MP, 0)).astype(jnp.bfloat16)
    grad_act = blocked(((upstream, down_eff),), N_SECTION, 1)
    grad_gate = (grad_act * up_pre * sigmoid_gate * (1.0 + gate_pre * (1.0 - sigmoid_gate))).astype(jnp.bfloat16)
    grad_up = (grad_act * gate_pre * sigmoid_gate).astype(jnp.bfloat16)
    down_grad = (jnp.dot(activation.T, upstream, preferred_element_type=jnp.float32) * expand(down_mask)).astype(jnp.bfloat16)
    gate_grad = (jnp.dot(normed.T, grad_gate, preferred_element_type=jnp.float32) * expand(gate_mask)).astype(jnp.bfloat16)
    up_grad = (jnp.dot(normed.T, grad_up, preferred_element_type=jnp.float32) * expand(up_mask)).astype(jnp.bfloat16)
    grad_normed = blocked(((grad_gate, gate_eff), (grad_up, up_eff)), N_MP, 1)
    grad_scaled = grad_normed * gain_f
    inner_mean = lax.optimization_barrier(jnp.mean(grad_scaled * scaled, axis=1, keepdims=True))
    input_grad = (upstream.astype(jnp.float32) + inv_rms * (grad_scaled - scaled * inner_mean)).astype(jnp.bfloat16)
    return (layer_out, input_grad, gate_grad, up_grad, down_grad)
```

```python
import jax
import jax.numpy as jnp
from jax import lax
from jax.experimental import pallas as pl
from jax.experimental.pallas import tpu as pltpu
from jax.sharding import PartitionSpec as P

D = 8192
BLOCK = 64
EPSILON = 1e-05

X_COUNT = 4
Z_COUNT = 8
OWN = 32
CHUNK = 128
CHUNKS = 4
TOKENS = 512
WIDTH = 512
HALF = 896
PACK = 3 * HALF + 128
BACK = 2 * WIDTH + 128

OFFSETS = ((-1, 2), (-2, 3), (-3, 4), (0, 1))
GROUP_ROW = {
    offset: CHUNK * chunk + 64 * place
    for chunk, pair in enumerate(OFFSETS)
    for place, offset in enumerate(pair)
}

ORDER = (
    (0, 1), (0, 2), (1, 0), (0, 3), (1, 1), (2, 0), (0, 4), (1, 2), (1, 3), (2, 1), (3, 0), (2, 2),
    (2, 3), (3, 1), (4, 0), (3, 2), (5, 0), (3, 3), (4, 1), (6, 0), (4, 2), (4, 3), (5, 1), (7, 0),
    (5, 2), (8, 0), (5, 3), (9, 0), (6, 1), (6, 2), (7, 1), (6, 3), (7, 2), (8, 1), (9, 1), (7, 3),
    (8, 2), (9, 2), (8, 3), (9, 3),
)
COPY_SLOTS = 160
LOCAL_SLOTS = 24


def dot(left_side, right_side, left_dim, right_dim):
    return lax.dot_general(
        left_side,
        right_side,
        (((left_dim,), (right_dim,)), ((), ())),
        preferred_element_type=jnp.float32,
    )


def lanes(rows):
    return lax.broadcasted_iota(jnp.int32, (rows, 128), 1)


def split_sum(total):
    high = total.astype(jnp.bfloat16).astype(jnp.float32)
    return high, total - high


def pack_sums(first, second=None):
    lane = lanes(first.shape[0])
    high, low = split_sum(first)
    packed = jnp.where(lane == 0, high, jnp.where(lane == 1, low, 0.0))
    if second is not None:
        high, low = split_sum(second)
        packed = jnp.where(lane == 2, high, jnp.where(lane == 3, low, packed))
    return packed.astype(jnp.bfloat16)


def unpack_sum(packed, first_lane):
    lane = lanes(packed.shape[0])
    kept = (lane == first_lane) | (lane == first_lane + 1)
    return jnp.sum(
        jnp.where(kept, packed.astype(jnp.float32), 0.0), axis=1, keepdims=True
    )


def widen_mask(marks, rows, cols, by_cols, first):
    marks_f = marks.astype(jnp.float32).astype(jnp.bfloat16)
    row = lax.broadcasted_iota(jnp.int32, (rows, cols), 0)
    col = lax.broadcasted_iota(jnp.int32, (rows, cols), 1) + first
    spread = jnp.where(row == (col >> 6), 1.0, 0.0).astype(jnp.bfloat16)
    return dot(marks_f, spread, 1, 0)


def kernel(
    tokens, upstream, gain, gate_w, up_w, down_w, gate_m, up_m, down_m,
    layer_out, input_grad, gate_grad, up_grad, down_grad,
    xt, gw, uw, dw, mg, mu, md, part, core_in, mid, near, far, summed, y_in, full, normed,
    back, back_in, grad_stage, send, recv, local,
):
    section = lax.axis_index("section")
    mp = lax.axis_index("mp")
    core = lax.rem(section, 2)
    x = lax.rem(lax.div(section, 2), X_COUNT)
    y_hi = lax.div(section, 2 * X_COUNT)
    y_lo = lax.div(mp, Z_COUNT)
    z = lax.rem(mp, Z_COUNT)

    def section_of(y_at, x_at, core_at):
        return (y_at * X_COUNT + x_at) * 2 + core_at

    x_up, x_down = lax.rem(x + 1, X_COUNT), lax.rem(x + 3, X_COUNT)
    x_far = lax.rem(x + 2, X_COUNT)
    to_core = (section_of(y_hi, x, 1 - core), mp)
    to_x_up = (section_of(y_hi, x_up, core), mp)
    to_x_down = (section_of(y_hi, x_down, core), mp)
    to_y = (section_of(1 - y_hi, x, core), mp)

    def mp_peer(line, offset):
        y_at = y_lo if line == 0 else 1 - y_lo
        return (section, y_at * Z_COUNT + lax.rem(z + offset + Z_COUNT, Z_COUNT))

    copies = []

    def remote(src, dst, device):
        slot = len(copies)
        copy = pltpu.make_async_remote_copy(
            src_ref=src,
            dst_ref=dst,
            send_sem=send.at[slot],
            recv_sem=recv.at[slot],
            device_id=device,
            device_id_type=pl.DeviceIdType.MESH,
        )
        copy.start()
        copies.append(copy)
        return copy

    local_count = [0]

    def nearby(src, dst):
        copy = pltpu.make_async_copy(src, dst, local.at[local_count[0]])
        local_count[0] += 1
        copy.start()
        return copy

    own_row = GROUP_ROW[0]
    own_rows = pl.ds(own_row, OWN)
    own_loads = [
        nearby(tokens, xt.at[own_rows, pl.ds(0, WIDTH)]),
        nearby(upstream, xt.at[own_rows, pl.ds(WIDTH, WIDTH)]),
    ]
    weight_loads = []
    for half in range(2):
        hidden = pl.ds(half * HALF, HALF)
        weight_loads.append(nearby(gate_w.at[:, hidden], gw.at[half]))
        weight_loads.append(nearby(up_w.at[:, hidden], uw.at[half]))
        weight_loads.append(nearby(down_w.at[hidden, :], dw.at[half]))

    partners = [to_core, to_x_up, to_x_down, to_y]
    for line in range(2):
        for offset in range(Z_COUNT):
            if line or offset:
                partners.append(mp_peer(line, offset))
    barrier = pltpu.get_barrier_semaphore()
    for partner in partners:
        pl.semaphore_signal(
            barrier, inc=1, device_id=partner, device_id_type=pl.DeviceIdType.MESH
        )
    for half in range(2):
        mg[half] = widen_mask(gate_m[...], 28, HALF, True, half * HALF)
        mu[half] = widen_mask(up_m[...], 28, HALF, True, half * HALF)
    md[...] = widen_mask(down_m[...], 8, WIDTH, True, 0)
    for load in own_loads:
        load.wait()
    pl.semaphore_wait(barrier, len(partners))

    def group(offset, first=0, rows=64):
        return xt.at[pl.ds(GROUP_ROW[offset] + first, rows), :]

    to_line = mp_peer(1, 0)
    to_z_up, to_z_down = mp_peer(0, 1), mp_peer(0, -1)
    line_copy = remote(group(0, 0, OWN), group(0, OWN, OWN), to_line)
    from_down = [remote(group(0, 0, OWN), group(-1, 0, OWN), to_z_up)]
    from_up = [remote(group(0, 0, OWN), group(1, 0, OWN), to_z_down)]

    gain_f = gain[...].astype(jnp.float32)

    for load in weight_loads:
        load.wait()

    for half in range(2):

        def mask_rows(block, carry):
            rows = pl.ds(pl.multiple_of(block * BLOCK, BLOCK), BLOCK)
            at = pl.ds(block, 1)
            gw[half, rows, :] = (gw[half, rows, :].astype(jnp.float32) * mg[half, at, :]).astype(
                jnp.bfloat16
            )
            uw[half, rows, :] = (uw[half, rows, :].astype(jnp.float32) * mu[half, at, :]).astype(
                jnp.bfloat16
            )
            return carry

        def mask_down_rows(block, carry):
            rows = pl.ds(pl.multiple_of(block * BLOCK, BLOCK), BLOCK)
            at = pl.ds(block + half * (HALF // BLOCK), 1)
            dw[half, rows, :] = (dw[half, rows, :].astype(jnp.float32) * md[at, :]).astype(
                jnp.bfloat16
            )
            return carry

        if half == 0:
            line_copy.wait_recv()
            from_down.append(remote(group(0, OWN, OWN), group(-1, OWN, OWN), to_z_up))
            from_up.append(remote(group(0, OWN, OWN), group(1, OWN, OWN), to_z_down))
        lax.fori_loop(0, WIDTH // BLOCK, mask_rows, 0)
        lax.fori_loop(0, HALF // BLOCK, mask_down_rows, 0)

    ring = {"down": from_down, "up": from_up}

    def ring_step(step):
        for copy in ring["down"] + ring["up"]:
            copy.wait_recv()
        if step < 3:
            ring["down"] = [remote(group(-step), group(-step - 1), to_z_up)]
            ring["up"] = [remote(group(step), group(step + 1), to_z_down)]
        elif step == 3:
            ring["down"] = [remote(group(-3, 0, OWN), group(4, 0, OWN), to_z_up)]
            ring["up"] = [remote(group(3, OWN, OWN), group(4, OWN, OWN), to_z_down)]

    pending = {}

    def row_of(chunk, x_at, first=0):
        return pl.multiple_of(chunk * CHUNK + x_at * 32 + first, 16)

    def products(chunk):
        rows = pl.ds(chunk * CHUNK, CHUNK)
        values = xt[rows, 0:WIDTH].astype(jnp.float32)
        gained = (values * gain_f).astype(jnp.bfloat16)
        back_values = xt[rows, WIDTH : 2 * WIDTH]
        sums = pack_sums(jnp.sum(values * values, axis=1, keepdims=True))
        for turn in range(2):
            half = 1 - core if turn == 0 else core
            part[half, rows, 0:HALF] = dot(gained, gw[half], 1, 0).astype(jnp.bfloat16)
            part[half, rows, HALF : 2 * HALF] = dot(gained, uw[half], 1, 0).astype(jnp.bfloat16)
            part[half, rows, 2 * HALF : 3 * HALF] = dot(back_values, dw[half], 1, 1).astype(
                jnp.bfloat16
            )
            part[half, rows, 3 * HALF :] = sums
            if turn == 0:
                pending["core", chunk] = remote(
                    part.at[half, rows, :], core_in.at[rows, :], to_core
                )

    def add_packed(left_side, right_side):
        left_f, right_f = left_side.astype(jnp.float32), right_side.astype(jnp.float32)
        return left_f + right_f

    def store_sum(ref, total_fn, rows):
        ref[..., 0 : 3 * HALF] = total_fn(slice(0, 3 * HALF)).astype(jnp.bfloat16)
        ref[..., 3 * HALF :] = pack_sums(unpack_sum(total_fn(slice(3 * HALF, PACK)), 0))

    def add_cores(chunk):
        pending["core", chunk].wait_recv()

        def add_rows(piece, carry):
            rows = pl.ds(pl.multiple_of(chunk * CHUNK + piece * 16, 16), 16)
            store_sum(
                part.at[core, rows, :],
                lambda cols: part[core, rows, cols].astype(jnp.float32)
                + core_in[rows, cols].astype(jnp.float32),
                16,
            )
            return carry

        lax.fori_loop(0, CHUNK // 16, add_rows, 0)
        low, high = pl.ds(0, 16), pl.ds(16, 16)

        def piece_of(x_at, first):
            return part.at[core, pl.ds(row_of(chunk, x_at, first), 16), :]

        pending["mid", chunk] = (
            remote(piece_of(x_far, 0), mid.at[chunk, low, :], to_x_up),
            remote(piece_of(x_far, 16), mid.at[chunk, high, :], to_x_down),
        )
        pending["near", chunk] = (
            remote(piece_of(x_up, 16), near.at[chunk, high, :], to_x_up),
            remote(piece_of(x_down, 0), near.at[chunk, low, :], to_x_down),
        )

    def add_middle(chunk):
        sent = []
        for place, (x_at, device) in enumerate(((x_up, to_x_up), (x_down, to_x_down))):
            pending["mid", chunk][place].wait_recv()
            here = pl.ds(place * 16, 16)
            rows = pl.ds(row_of(chunk, x_at, place * 16), 16)
            store_sum(
                part.at[core, rows, :],
                lambda cols: part[core, rows, cols].astype(jnp.float32)
                + mid[chunk, here, cols].astype(jnp.float32),
                16,
            )
            sent.append(remote(part.at[core, rows, :], far.at[chunk, here, :], device))
        pending["far", chunk] = sent

    def add_line(chunk):
        for copy in (*pending["near", chunk], *pending["far", chunk]):
            copy.wait_recv()
        rows = pl.ds(row_of(chunk, x), 32)
        store_sum(
            summed.at[chunk],
            lambda cols: part[core, rows, cols].astype(jnp.float32)
            + near[chunk, :, cols].astype(jnp.float32)
            + far[chunk, :, cols].astype(jnp.float32),
            32,
        )
        other = pl.ds(pl.multiple_of((1 - y_hi) * 16, 16), 16)
        pending["y", chunk] = remote(summed.at[chunk, other, :], y_in.at[chunk], to_y)

    def activate(chunk):
        pending["y", chunk].wait_recv()
        kept = pl.ds(pl.multiple_of(y_hi * 16, 16), 16)

        def total(first, last):
            return summed[chunk, kept, first:last].astype(jnp.float32) + y_in[
                chunk, :, first:last
            ].astype(jnp.float32)

        squares = unpack_sum(total(3 * HALF, PACK), 0)
        inv_rms = lax.rsqrt(squares / D + EPSILON)
        gate_pre = total(0, HALF) * inv_rms
        up_pre = total(HALF, 2 * HALF) * inv_rms
        grad_act = total(2 * HALF, 3 * HALF)
        sigmoid_gate = jax.nn.sigmoid(gate_pre)
        gated = gate_pre * sigmoid_gate
        grad_gate = (
            grad_act * up_pre * sigmoid_gate * (1.0 + gate_pre * (1.0 - sigmoid_gate))
        ).astype(jnp.bfloat16)
        grad_up = (grad_act * gated).astype(jnp.bfloat16)
        inner = jnp.sum(
            grad_gate.astype(jnp.float32) * gate_pre + grad_up.astype(jnp.float32) * up_pre,
            axis=1,
            keepdims=True,
        )
        rows = pl.ds(row_of(chunk, x, y_hi * 16), 16)
        full[core, rows, 0:HALF] = (gated * up_pre).astype(jnp.bfloat16)
        full[core, rows, HALF : 2 * HALF] = grad_gate
        full[core, rows, 2 * HALF : 3 * HALF] = grad_up
        full[core, rows, 3 * HALF :] = pack_sums(inv_rms, inner)
        piece = full.at[core, rows, :]
        pending["y_back", chunk] = remote(piece, piece, to_y)

    def full_rows(chunk, x_at, first, rows):
        return full.at[core, pl.ds(row_of(chunk, x_at, first), rows), :]

    def same_place(piece, device):
        return remote(piece, piece, device)

    def gather_own(chunk):
        pending["y_back", chunk].wait_recv()
        piece = full_rows(chunk, x, 0, 32)
        pending["x_back", chunk] = (same_place(piece, to_x_up), same_place(piece, to_x_down))
        pending["core_back", chunk] = [same_place(piece, to_core)]

    def gather_near(chunk):
        for copy in pending["x_back", chunk]:
            copy.wait_recv()
        pending["x_far", chunk] = (
            same_place(full_rows(chunk, x_down, 0, 16), to_x_up),
            same_place(full_rows(chunk, x_up, 16, 16), to_x_down),
        )
        pending["core_back", chunk].append(same_place(full_rows(chunk, x_down, 0, 32), to_core))
        pending["core_back", chunk].append(same_place(full_rows(chunk, x_up, 0, 32), to_core))

    def gather_far(chunk):
        for copy in pending["x_far", chunk]:
            copy.wait_recv()
        pending["core_back", chunk].append(same_place(full_rows(chunk, x_far, 0, 32), to_core))

    def finish(chunk):
        for copy in pending["core_back", chunk]:
            copy.wait_recv()
        rows = pl.ds(chunk * CHUNK, CHUNK)
        down_sum = dot(full[0, rows, 0:HALF], dw[0], 1, 0) + dot(
            full[1, rows, 0:HALF], dw[1], 1, 0
        )
        back[rows, 0:WIDTH] = down_sum.astype(jnp.bfloat16)
        grad_sum = (
            dot(full[0, rows, HALF : 2 * HALF], gw[0], 1, 1)
            + dot(full[1, rows, HALF : 2 * HALF], gw[1], 1, 1)
            + dot(full[0, rows, 2 * HALF : 3 * HALF], uw[0], 1, 1)
            + dot(full[1, rows, 2 * HALF : 3 * HALF], uw[1], 1, 1)
        )
        back[rows, WIDTH : 2 * WIDTH] = grad_sum.astype(jnp.bfloat16)
        sums = full[0, rows, 3 * HALF :]
        back[rows, 2 * WIDTH :] = pack_sums(
            unpack_sum(sums, 2) + unpack_sum(full[1, rows, 3 * HALF :], 2)
        )
        for place, offset in enumerate(OFFSETS[chunk]):
            for line in range(2):
                if offset == 0 and line == 0:
                    continue
                first = chunk * CHUNK + place * 64 + line * OWN
                pending["back", line, offset] = remote(
                    back.at[pl.ds(first, OWN), :],
                    back_in.at[line * Z_COUNT + offset % Z_COUNT],
                    mp_peer(line, offset),
                )
        inv_rms = unpack_sum(sums, 0)
        normed[rows, :] = (xt[rows, 0:WIDTH].astype(jnp.float32) * inv_rms * gain_f).astype(
            jnp.bfloat16
        )

    stages = (
        None, products, add_cores, add_middle, add_line, activate, gather_own, gather_near,
        gather_far, finish,
    )
    for stage, which in ORDER:
        if stage == 0:
            ring_step(which)
        else:
            stages[stage](which)

    stores = []
    upstream_full = xt[:, WIDTH : 2 * WIDTH]
    for half in range(2):
        hidden = pl.ds(half * HALF, HALF)
        activation = full[half, :, 0:HALF]
        grads = dot(activation, upstream_full, 0, 0)
        for block in range(HALF // BLOCK):
            rows = slice(block * BLOCK, (block + 1) * BLOCK)
            mark = half * (HALF // BLOCK) + block
            grad_stage[2, pl.ds(half * HALF + block * BLOCK, BLOCK), 0:WIDTH] = (
                grads[rows, :] * md[mark : mark + 1, :]
            ).astype(jnp.bfloat16)
        stores.append(
            nearby(grad_stage.at[2, hidden, pl.ds(0, WIDTH)], down_grad.at[hidden, :])
        )
        for which, marks, target in ((0, mg, gate_grad), (1, mu, up_grad)):
            first = (1 + which) * HALF
            grads = dot(normed[...], full[half, :, first : first + HALF], 0, 0)
            for block in range(WIDTH // BLOCK):
                rows = slice(block * BLOCK, (block + 1) * BLOCK)
                grad_stage[which, pl.ds(half * WIDTH + block * BLOCK, BLOCK), :] = (
                    grads[rows, :] * marks[half, block : block + 1, :]
                ).astype(jnp.bfloat16)
            stores.append(
                nearby(
                    grad_stage.at[which, pl.ds(half * WIDTH, WIDTH), :], target.at[:, hidden]
                )
            )

    total = back[own_rows, :].astype(jnp.float32)
    for line in range(2):
        for offset in (0, 1, -1, 2, -2, 3, -3, 4):
            if line or offset:
                pending["back", line, offset].wait_recv()
                total = total + back_in[line * Z_COUNT + offset % Z_COUNT].astype(jnp.float32)
    inputs_f = xt[own_rows, 0:WIDTH].astype(jnp.float32)
    layer_out[...] = (inputs_f + total[:, 0:WIDTH]).astype(jnp.bfloat16)
    inner_mean = unpack_sum(total[:, 2 * WIDTH :], 0) / D
    inv_rms = unpack_sum(full[0, own_rows, 3 * HALF :], 0)
    grad_scaled = total[:, WIDTH : 2 * WIDTH] * gain_f
    input_grad[...] = (
        xt[own_rows, WIDTH : 2 * WIDTH].astype(jnp.float32)
        + inv_rms * (grad_scaled - inputs_f * inv_rms * inner_mean)
    ).astype(jnp.bfloat16)

    for copy in copies:
        copy.wait_send()
    for store in stores:
        store.wait()


def on_device(
    tokens, upstream, norm_gain, gate_weight, up_weight, down_weight, gate_mask, up_mask, down_mask
):
    in_vmem = pl.BlockSpec(memory_space=pltpu.VMEM)
    anywhere = pl.BlockSpec(memory_space=pl.ANY)
    bf16 = jnp.bfloat16
    return pl.pallas_call(
        kernel,
        out_shape=(
            jax.ShapeDtypeStruct((OWN, WIDTH), bf16),
            jax.ShapeDtypeStruct((OWN, WIDTH), bf16),
            jax.ShapeDtypeStruct((WIDTH, 2 * HALF), bf16),
            jax.ShapeDtypeStruct((WIDTH, 2 * HALF), bf16),
            jax.ShapeDtypeStruct((2 * HALF, WIDTH), bf16),
        ),
        in_specs=[anywhere, anywhere, in_vmem] + [anywhere] * 3 + [in_vmem] * 3,
        out_specs=[in_vmem, in_vmem, anywhere, anywhere, anywhere],
        scratch_shapes=[
            pltpu.VMEM((TOKENS, 2 * WIDTH), bf16),
            pltpu.VMEM((2, WIDTH, HALF), bf16),
            pltpu.VMEM((2, WIDTH, HALF), bf16),
            pltpu.VMEM((2, HALF, WIDTH), bf16),
            pltpu.VMEM((2, 8, HALF), jnp.float32),
            pltpu.VMEM((2, 8, HALF), jnp.float32),
            pltpu.VMEM((28, WIDTH), jnp.float32),
            pltpu.VMEM((2, TOKENS, PACK), bf16),
            pltpu.VMEM((TOKENS, PACK), bf16),
            pltpu.VMEM((CHUNKS, 32, PACK), bf16),
            pltpu.VMEM((CHUNKS, 32, PACK), bf16),
            pltpu.VMEM((CHUNKS, 32, PACK), bf16),
            pltpu.VMEM((CHUNKS, 32, PACK), bf16),
            pltpu.VMEM((CHUNKS, 16, PACK), bf16),
            pltpu.VMEM((2, TOKENS, PACK), bf16),
            pltpu.VMEM((TOKENS, WIDTH), bf16),
            pltpu.VMEM((TOKENS, BACK), bf16),
            pltpu.VMEM((16, OWN, BACK), bf16),
            pltpu.VMEM((3, 2 * HALF, HALF), bf16),
            pltpu.SemaphoreType.DMA((COPY_SLOTS,)),
            pltpu.SemaphoreType.DMA((COPY_SLOTS,)),
            pltpu.SemaphoreType.DMA((LOCAL_SLOTS,)),
        ],
        compiler_params=pltpu.CompilerParams(
            collective_id=0, has_side_effects=True, vmem_limit_bytes=56 * 1024 * 1024
        ),
    )(
        tokens, upstream, norm_gain.reshape(1, WIDTH), gate_weight, up_weight, down_weight,
        gate_mask, up_mask, down_mask,
    )


def solution(mesh):
    in_specs = (
        P("mp", "section"),
        P("mp", "section"),
        P("section"),
        P("section", "mp"),
        P("section", "mp"),
        P("mp", "section"),
        P("section", "mp"),
        P("section", "mp"),
        P("mp", "section"),
    )
    out_specs = (
        P("mp", "section"),
        P("mp", "section"),
        P("section", "mp"),
        P("section", "mp"),
        P("mp", "section"),
    )
    return jax.shard_map(
        on_device, mesh=mesh, in_specs=in_specs, out_specs=out_specs, check_vma=False
    )
```

```python
import jax
import jax.numpy as jnp
from jax import lax
from jax.experimental import pallas as pl
from jax.experimental.pallas import tpu as pltpu
from jax.sharding import PartitionSpec as P

D = 8192
BLOCK = 64
EPSILON = 1e-05

X_COUNT = 4
Z_COUNT = 8
OWN = 32
CHUNK = 128
CHUNKS = 4
TOKENS = 512
WIDTH = 512
HALF = 896
PACK = 3 * HALF + 128
BACK = 2 * WIDTH + 128

OFFSETS = ((0, 1), (-1, 2), (-2, 3), (-3, 4))
GROUP_ROW = {
    offset: CHUNK * chunk + 64 * place
    for chunk, pair in enumerate(OFFSETS)
    for place, offset in enumerate(pair)
}
LINE_FIRST = (False, True, False, True)
LINE_BUFFER = (0, 0, 0, 1)
COLUMNS = ((0, PACK // 2), (PACK // 2, PACK // 2))

ORDER = (
    (0, 1), (1, 0), (0, 2), (1, 1), (2, 0), (0, 3), (2, 1), (1, 2), (3, 0), (0, 4), (2, 2), (1, 3),
    (4, 0), (2, 3), (3, 1), (5, 0), (4, 1), (3, 2), (5, 1), (4, 2), (3, 3), (6, 1), (5, 2), (4, 3),
    (7, 1), (6, 2), (5, 3), (6, 0), (8, 1), (7, 2), (6, 3), (9, 1), (8, 2), (7, 3), (7, 0), (9, 2),
    (8, 3), (8, 0), (9, 3), (9, 0),
)
COPY_SLOTS = 192
LOCAL_SLOTS = 24


def dot(left_side, right_side, left_dim, right_dim):
    return lax.dot_general(
        left_side,
        right_side,
        (((left_dim,), (right_dim,)), ((), ())),
        preferred_element_type=jnp.float32,
    )


def lanes(rows):
    return lax.broadcasted_iota(jnp.int32, (rows, 128), 1)


def split_sum(total):
    high = total.astype(jnp.bfloat16).astype(jnp.float32)
    return high, total - high


def pack_sums(first, second=None):
    lane = lanes(first.shape[0])
    high, low = split_sum(first)
    packed = jnp.where(lane == 0, high, jnp.where(lane == 1, low, 0.0))
    if second is not None:
        high, low = split_sum(second)
        packed = jnp.where(lane == 2, high, jnp.where(lane == 3, low, packed))
    return packed.astype(jnp.bfloat16)


def unpack_sum(packed, first_lane):
    lane = lanes(packed.shape[0])
    kept = (lane == first_lane) | (lane == first_lane + 1)
    return jnp.sum(
        jnp.where(kept, packed.astype(jnp.float32), 0.0), axis=1, keepdims=True
    )


def widen_mask(marks, rows, cols, first=0, marks_dim=1):
    marks_f = marks.astype(jnp.float32).astype(jnp.bfloat16)
    row = lax.broadcasted_iota(jnp.int32, (rows, cols), 0)
    col = lax.broadcasted_iota(jnp.int32, (rows, cols), 1) + first
    spread = jnp.where(row == (col >> 6), 1.0, 0.0).astype(jnp.bfloat16)
    return dot(marks_f, spread, marks_dim, 0)


def kernel(
    tokens, upstream, gain, gate_w, up_w, down_w, gate_m, up_m, down_m,
    layer_out, input_grad, xt, full, normed,
    gw, uw, dw, mg, mu, md, part, core_in, mid, near, far, summed, y_in, line_in,
    back, back_in, send, recv, local,
):
    section = lax.axis_index("section")
    mp = lax.axis_index("mp")
    core = lax.rem(section, 2)
    x = lax.rem(lax.div(section, 2), X_COUNT)
    y_hi = lax.div(section, 2 * X_COUNT)
    y_lo = lax.div(mp, Z_COUNT)
    z = lax.rem(mp, Z_COUNT)

    def section_of(y_at, x_at, core_at):
        return (y_at * X_COUNT + x_at) * 2 + core_at

    x_up, x_down = lax.rem(x + 1, X_COUNT), lax.rem(x + 3, X_COUNT)
    x_far = lax.rem(x + 2, X_COUNT)
    to_core = (section_of(y_hi, x, 1 - core), mp)
    to_x_up = (section_of(y_hi, x_up, core), mp)
    to_x_down = (section_of(y_hi, x_down, core), mp)
    to_y = (section_of(1 - y_hi, x, core), mp)

    def mp_peer(line, offset):
        y_at = y_lo if line == 0 else 1 - y_lo
        return (section, y_at * Z_COUNT + lax.rem(z + offset + Z_COUNT, Z_COUNT))

    copies = []

    def remote(src, dst, device):
        slot = len(copies)
        copy = pltpu.make_async_remote_copy(
            src_ref=src,
            dst_ref=dst,
            send_sem=send.at[slot],
            recv_sem=recv.at[slot],
            device_id=device,
            device_id_type=pl.DeviceIdType.MESH,
        )
        copy.start()
        copies.append(copy)
        return copy

    local_count = [0]

    def nearby(src, dst):
        copy = pltpu.make_async_copy(src, dst, local.at[local_count[0]])
        local_count[0] += 1
        copy.start()
        return copy

    own_row = GROUP_ROW[0]
    own_rows = pl.ds(own_row, OWN)
    own_loads = [
        nearby(tokens, xt.at[own_rows, pl.ds(0, WIDTH)]),
        nearby(upstream, xt.at[own_rows, pl.ds(WIDTH, WIDTH)]),
    ]
    weight_loads = []
    for half in range(2):
        hidden = pl.ds(half * HALF, HALF)
        weight_loads.append(nearby(gate_w.at[:, hidden], gw.at[half]))
        weight_loads.append(nearby(up_w.at[:, hidden], uw.at[half]))
        weight_loads.append(nearby(down_w.at[hidden, :], dw.at[half]))

    to_line = mp_peer(1, 0)
    partners = [to_line]
    for offset in (1, -1, 2, -2):
        partners += [mp_peer(0, offset), mp_peer(1, offset)]
    partners += [to_core, to_x_up, to_x_down, to_y]
    barrier = pltpu.get_barrier_semaphore()
    for partner in partners:
        pl.semaphore_signal(
            barrier, inc=1, device_id=partner, device_id_type=pl.DeviceIdType.MESH
        )
    for load in own_loads:
        load.wait()
    pl.semaphore_wait(barrier, len(partners))

    def group(offset, first=0, rows=64):
        return xt.at[pl.ds(GROUP_ROW[offset] + first, rows), :]

    def send_own(line, offset):
        return remote(
            group(0, 0, OWN), group(-offset, line * OWN, OWN), mp_peer(line, offset)
        )

    arriving = {0: [send_own(1, 0)]}
    for offset in (1, -1, 2, -2):
        arriving[-offset] = [send_own(0, offset), send_own(1, offset)]

    gain_f = gain[...].astype(jnp.float32).reshape(1, WIDTH)
    for half in range(2):
        mg[half] = widen_mask(gate_m[...], 28, HALF, half * HALF)
        mu[half] = widen_mask(up_m[...], 28, HALF, half * HALF)
    md[...] = widen_mask(down_m[...], 8, WIDTH, 0, 0)

    for load in weight_loads:
        load.wait()

    for half in range(2):

        def mask_rows(block, carry):
            rows = pl.ds(pl.multiple_of(block * BLOCK, BLOCK), BLOCK)
            at = pl.ds(block, 1)
            gw[half, rows, :] = (gw[half, rows, :].astype(jnp.float32) * mg[half, at, :]).astype(
                jnp.bfloat16
            )
            uw[half, rows, :] = (uw[half, rows, :].astype(jnp.float32) * mu[half, at, :]).astype(
                jnp.bfloat16
            )
            return carry

        def mask_down_rows(block, carry):
            rows = pl.ds(pl.multiple_of(block * BLOCK, BLOCK), BLOCK)
            at = pl.ds(block + half * (HALF // BLOCK), 1)
            dw[half, rows, :] = (dw[half, rows, :].astype(jnp.float32) * md[at, :]).astype(
                jnp.bfloat16
            )
            return carry

        lax.fori_loop(0, WIDTH // BLOCK, mask_rows, 0)
        lax.fori_loop(0, HALF // BLOCK, mask_down_rows, 0)

    def token_step(step):
        for offset in (0, 1, -1) if step == 1 else (step, -step) if step < 4 else (4,):
            for copy in arriving[offset]:
                copy.wait_recv()
        if step == 1:
            arriving[-3] = [remote(group(-1), group(-3), mp_peer(0, 2))]
            arriving[3] = [remote(group(1), group(3), mp_peer(0, -2))]
        elif step == 2:
            arriving[4] = [
                remote(group(-2, 0, OWN), group(4, 0, OWN), mp_peer(0, 2)),
                remote(group(2, OWN, OWN), group(4, OWN, OWN), mp_peer(0, -2)),
            ]

    pending = {}

    def row_of(chunk, x_at, y_at=0):
        if LINE_FIRST[chunk]:
            return pl.multiple_of(chunk * CHUNK + y_at * 64 + x_at * 16, 16)
        return pl.multiple_of(chunk * CHUNK + x_at * 32 + y_at * 16, 16)

    def line_rows(chunk, y_at):
        return pl.ds(pl.multiple_of(chunk * CHUNK + y_at * 64, 64), 64)

    def products(chunk):
        rows = pl.ds(chunk * CHUNK, CHUNK)
        values = xt[rows, 0:WIDTH].astype(jnp.float32)
        gained = (values * gain_f).astype(jnp.bfloat16)
        back_values = xt[rows, WIDTH : 2 * WIDTH]
        sums = pack_sums(jnp.sum(values * values, axis=1, keepdims=True))
        for turn in range(2):
            half = 1 - core if turn == 0 else core
            part[half, rows, 0:HALF] = dot(gained, gw[half], 1, 0).astype(jnp.bfloat16)
            part[half, rows, HALF : 2 * HALF] = dot(gained, uw[half], 1, 0).astype(jnp.bfloat16)
            part[half, rows, 2 * HALF : 3 * HALF] = dot(back_values, dw[half], 1, 1).astype(
                jnp.bfloat16
            )
            part[half, rows, 3 * HALF :] = sums
            if turn == 0:
                pending["core", chunk] = remote(
                    part.at[half, rows, :], core_in.at[rows, :], to_core
                )

    def store_sum(ref, total_fn):
        ref[..., 0 : 3 * HALF] = total_fn(slice(0, 3 * HALF)).astype(jnp.bfloat16)
        ref[..., 3 * HALF :] = pack_sums(unpack_sum(total_fn(slice(3 * HALF, PACK)), 0))

    def add_pieces(first_row, count, source, source_row):
        def add_rows(piece, carry):
            rows = pl.ds(pl.multiple_of(first_row + piece * 16, 16), 16)
            source_rows = pl.ds(pl.multiple_of(source_row + piece * 16, 16), 16)
            store_sum(
                part.at[core, rows, :],
                lambda cols: part[core, rows, cols].astype(jnp.float32)
                + source[source_rows, cols].astype(jnp.float32),
            )
            return carry

        lax.fori_loop(0, count, add_rows, 0)

    def x_part(chunk, x_at):
        if LINE_FIRST[chunk]:
            return pl.ds(row_of(chunk, x_at, y_hi), 16)
        return pl.ds(row_of(chunk, x_at), 32)

    def part_size(chunk):
        return 16 if LINE_FIRST[chunk] else 32

    def start_ring(chunk):
        rows = pl.ds(0, part_size(chunk))

        def columns(x_at, turn, target, device):
            cols = pl.ds(*COLUMNS[turn])
            return remote(
                part.at[core, x_part(chunk, x_at), cols], target.at[chunk, rows, cols], device
            )

        pending["mid", chunk] = (
            columns(x_far, 0, mid, to_x_up), columns(x_far, 1, mid, to_x_down)
        )
        pending["near", chunk] = (
            columns(x_up, 1, near, to_x_up), columns(x_down, 0, near, to_x_down)
        )

    def turn_ring(chunk):
        here = pl.ds(0, part_size(chunk))
        sent = []
        for turn, (x_at, device) in enumerate(((x_up, to_x_up), (x_down, to_x_down))):
            pending["mid", chunk][turn].wait_recv()
            rows = x_part(chunk, x_at)
            first, width = COLUMNS[turn]
            plain = width if turn == 0 else width - 128
            cols = slice(first, first + plain)
            part[core, rows, cols] = (
                part[core, rows, cols].astype(jnp.float32)
                + mid[chunk, here, cols].astype(jnp.float32)
            ).astype(jnp.bfloat16)
            if turn == 1:
                cols = slice(3 * HALF, PACK)
                part[core, rows, cols] = pack_sums(
                    unpack_sum(part[core, rows, cols], 0) + unpack_sum(mid[chunk, here, cols], 0)
                )
            cols = pl.ds(first, width)
            sent.append(remote(part.at[core, rows, cols], far.at[chunk, here, cols], device))
        pending["far", chunk] = sent

    def ring_total(chunk, cols):
        here = slice(0, part_size(chunk))
        return (
            part[core, x_part(chunk, x), cols].astype(jnp.float32)
            + near[chunk, here, cols].astype(jnp.float32)
            + far[chunk, here, cols].astype(jnp.float32)
        )

    def wait_ring(chunk):
        for copy in (*pending["near", chunk], *pending["far", chunk]):
            copy.wait_recv()

    def add_cores(chunk):
        pending["core", chunk].wait_recv()
        add_pieces(chunk * CHUNK, CHUNK // 16, core_in, chunk * CHUNK)
        if LINE_FIRST[chunk]:
            pending["line", chunk] = remote(
                part.at[core, line_rows(chunk, 1 - y_hi), :],
                line_in.at[LINE_BUFFER[chunk]],
                to_y,
            )
        else:
            start_ring(chunk)

    def third(chunk):
        if LINE_FIRST[chunk]:
            pending["line", chunk].wait_recv()
            add_pieces(
                chunk * CHUNK + y_hi * 64, 4, line_in.at[LINE_BUFFER[chunk]], 0
            )
            start_ring(chunk)
        else:
            turn_ring(chunk)

    def fourth(chunk):
        if LINE_FIRST[chunk]:
            turn_ring(chunk)
            return
        wait_ring(chunk)
        store_sum(summed.at[chunk], lambda cols: ring_total(chunk, cols))
        other = pl.ds(pl.multiple_of((1 - y_hi) * 16, 16), 16)
        pending["y", chunk] = remote(summed.at[chunk, other, :], y_in.at[chunk], to_y)

    def activate(chunk):
        if LINE_FIRST[chunk]:
            wait_ring(chunk)
        else:
            pending["y", chunk].wait_recv()
        kept = pl.ds(pl.multiple_of(y_hi * 16, 16), 16)

        def total(first, last):
            if LINE_FIRST[chunk]:
                return ring_total(chunk, slice(first, last))
            return summed[chunk, kept, first:last].astype(jnp.float32) + y_in[
                chunk, :, first:last
            ].astype(jnp.float32)

        squares = unpack_sum(total(3 * HALF, PACK), 0)
        inv_rms = lax.rsqrt(squares / D + EPSILON)
        gate_pre = total(0, HALF) * inv_rms
        up_pre = total(HALF, 2 * HALF) * inv_rms
        grad_act = total(2 * HALF, 3 * HALF)
        sigmoid_gate = jax.nn.sigmoid(gate_pre)
        gated = gate_pre * sigmoid_gate
        grad_gate = (
            grad_act * up_pre * sigmoid_gate * (1.0 + gate_pre * (1.0 - sigmoid_gate))
        ).astype(jnp.bfloat16)
        grad_up = (grad_act * gated).astype(jnp.bfloat16)
        inner = jnp.sum(
            grad_gate.astype(jnp.float32) * gate_pre + grad_up.astype(jnp.float32) * up_pre,
            axis=1,
            keepdims=True,
        )
        rows = pl.ds(row_of(chunk, x, y_hi), 16)
        full[core, rows, 0:HALF] = (gated * up_pre).astype(jnp.bfloat16)
        full[core, rows, HALF : 2 * HALF] = grad_gate
        full[core, rows, 2 * HALF : 3 * HALF] = grad_up
        full[core, rows, 3 * HALF :] = pack_sums(inv_rms, inner)
        piece = full.at[core, rows, :]
        pending["y_back", chunk] = [same_place(piece, to_y)]
        pending["x_back", chunk] = [same_place(piece, to_x_up), same_place(piece, to_x_down)]
        pending["core_back", chunk] = []

    def same_place(piece, device):
        return remote(piece, piece, device)

    def full_rows(chunk, x_at, y_at, rows=16, turn=None):
        cols = pl.ds(0, PACK) if turn is None else pl.ds(*COLUMNS[turn])
        return full.at[core, pl.ds(row_of(chunk, x_at, y_at), rows), cols]

    def to_other_core(chunk, piece):
        pending["core_back", chunk].append(same_place(piece, to_core))

    def wait_all(key, chunk):
        for copy in pending[key, chunk]:
            copy.wait_recv()

    def sixth(chunk):
        if LINE_FIRST[chunk]:
            wait_all("x_back", chunk)
            pending["x_far", chunk] = (
                same_place(full_rows(chunk, x_down, y_hi, 16, 0), to_x_up),
                same_place(full_rows(chunk, x_up, y_hi, 16, 1), to_x_down),
            )
            for x_at in (x_down, x_up):
                pending["y_back", chunk].append(
                    same_place(full_rows(chunk, x_at, y_hi), to_y)
                )
        else:
            wait_all("y_back", chunk)
            piece = full_rows(chunk, x, 1 - y_hi)
            pending["x_back", chunk] += [
                same_place(piece, to_x_up), same_place(piece, to_x_down)
            ]
            to_other_core(chunk, full_rows(chunk, x, 0, 32))

    def seventh(chunk):
        if LINE_FIRST[chunk]:
            wait_all("x_far", chunk)
            pending["y_back", chunk].append(
                same_place(full_rows(chunk, x_far, y_hi), to_y)
            )
            to_other_core(chunk, full.at[core, line_rows(chunk, y_hi), :])
        else:
            wait_all("x_back", chunk)
            pending["x_far", chunk] = (
                same_place(full_rows(chunk, x_down, 0, 32, 0), to_x_up),
                same_place(full_rows(chunk, x_up, 0, 32, 1), to_x_down),
            )
            to_other_core(chunk, full_rows(chunk, x_down, 0, 32))
            to_other_core(chunk, full_rows(chunk, x_up, 0, 32))

    def eighth(chunk):
        if LINE_FIRST[chunk]:
            wait_all("y_back", chunk)
            to_other_core(chunk, full.at[core, line_rows(chunk, 1 - y_hi), :])
        else:
            wait_all("x_far", chunk)
            to_other_core(chunk, full_rows(chunk, x_far, 0, 32))

    def finish(chunk):
        for copy in pending["core_back", chunk]:
            copy.wait_recv()
        rows = pl.ds(chunk * CHUNK, CHUNK)
        down_sum = dot(full[0, rows, 0:HALF], dw[0], 1, 0) + dot(
            full[1, rows, 0:HALF], dw[1], 1, 0
        )
        back[rows, 0:WIDTH] = down_sum.astype(jnp.bfloat16)
        grad_sum = (
            dot(full[0, rows, HALF : 2 * HALF], gw[0], 1, 1)
            + dot(full[1, rows, HALF : 2 * HALF], gw[1], 1, 1)
            + dot(full[0, rows, 2 * HALF : 3 * HALF], uw[0], 1, 1)
            + dot(full[1, rows, 2 * HALF : 3 * HALF], uw[1], 1, 1)
        )
        back[rows, WIDTH : 2 * WIDTH] = grad_sum.astype(jnp.bfloat16)
        sums = full[0, rows, 3 * HALF :]
        back[rows, 2 * WIDTH :] = pack_sums(
            unpack_sum(sums, 2) + unpack_sum(full[1, rows, 3 * HALF :], 2)
        )
        for place, offset in enumerate(OFFSETS[chunk]):
            for line in range(2):
                if offset == 0 and line == 0:
                    continue
                first = chunk * CHUNK + place * 64 + line * OWN
                pending["back", line, offset] = remote(
                    back.at[pl.ds(first, OWN), :],
                    back_in.at[line * Z_COUNT + offset % Z_COUNT],
                    mp_peer(line, offset),
                )
        inv_rms = unpack_sum(sums, 0)
        normed[rows, :] = (xt[rows, 0:WIDTH].astype(jnp.float32) * inv_rms * gain_f).astype(
            jnp.bfloat16
        )

    stages = (
        token_step, products, add_cores, third, fourth, activate, sixth, seventh, eighth, finish,
    )
    for stage, which in ORDER:
        stages[stage](which)

    total = back[own_rows, :].astype(jnp.float32)
    for line in range(2):
        for offset in (0, 1, -1, 2, -2, 3, -3, 4):
            if line or offset:
                pending["back", line, offset].wait_recv()
                total = total + back_in[line * Z_COUNT + offset % Z_COUNT].astype(jnp.float32)
    inputs_f = xt[own_rows, 0:WIDTH].astype(jnp.float32)
    layer_out[...] = (inputs_f + total[:, 0:WIDTH]).astype(jnp.bfloat16)
    inner_mean = unpack_sum(total[:, 2 * WIDTH :], 0) / D
    inv_rms = unpack_sum(full[0, own_rows, 3 * HALF :], 0)
    grad_scaled = total[:, WIDTH : 2 * WIDTH] * gain_f
    input_grad[...] = (
        xt[own_rows, WIDTH : 2 * WIDTH].astype(jnp.float32)
        + inv_rms * (grad_scaled - inputs_f * inv_rms * inner_mean)
    ).astype(jnp.bfloat16)

    for copy in copies:
        copy.wait_send()


def weight_kernel(
    sums_out, sums_in, xt, full, normed, gate_m, up_m, down_m,
    layer_out, input_grad, gate_grad, up_grad, down_grad,
    gate_stage, up_stage, down_stage, local,
):
    layer_out[...] = sums_out[...]
    input_grad[...] = sums_in[...]
    marks_d = widen_mask(down_m[...], 8, WIDTH, 0, 0)
    upstream_full = xt[:, WIDTH : 2 * WIDTH]
    stores = []

    def store(src, dst):
        copy = pltpu.make_async_copy(src, dst, local.at[len(stores)])
        copy.start()
        stores.append(copy)

    for half in range(2):
        hidden = pl.ds(half * HALF, HALF)
        grads = dot(full[half, :, 0:HALF], upstream_full, 0, 0)
        for block in range(HALF // BLOCK):
            rows = slice(block * BLOCK, (block + 1) * BLOCK)
            mark = half * (HALF // BLOCK) + block
            down_stage[half, rows, :] = (
                grads[rows, :] * marks_d[mark : mark + 1, :]
            ).astype(jnp.bfloat16)
        store(down_stage.at[half], down_grad.at[hidden, :])
        for which, stage, given, target in (
            (0, gate_stage, gate_m, gate_grad), (1, up_stage, up_m, up_grad)
        ):
            first = (1 + which) * HALF
            marks = widen_mask(given[...], 28, HALF, half * HALF)
            grads = dot(normed[...], full[half, :, first : first + HALF], 0, 0)
            for block in range(WIDTH // BLOCK):
                rows = slice(block * BLOCK, (block + 1) * BLOCK)
                stage[half, rows, :] = (grads[rows, :] * marks[block : block + 1, :]).astype(
                    jnp.bfloat16
                )
            store(stage.at[half], target.at[:, hidden])
    for copy in stores:
        copy.wait()


def on_device(
    tokens, upstream, norm_gain, gate_weight, up_weight, down_weight, gate_mask, up_mask, down_mask
):
    in_vmem = pl.BlockSpec(memory_space=pltpu.VMEM)
    anywhere = pl.BlockSpec(memory_space=pl.ANY)
    bf16 = jnp.bfloat16
    down_marks = down_mask.T
    sums_out, sums_in, xt, full, normed = pl.pallas_call(
        kernel,
        out_shape=(
            pltpu.VMEM((OWN, WIDTH), bf16),
            pltpu.VMEM((OWN, WIDTH), bf16),
            pltpu.VMEM((TOKENS, 2 * WIDTH), bf16),
            pltpu.VMEM((2, TOKENS, PACK), bf16),
            pltpu.VMEM((TOKENS, WIDTH), bf16),
        ),
        in_specs=[anywhere, anywhere, in_vmem] + [anywhere] * 3 + [in_vmem] * 3,
        out_specs=[in_vmem] * 5,
        scratch_shapes=[
            pltpu.VMEM((2, WIDTH, HALF), bf16),
            pltpu.VMEM((2, WIDTH, HALF), bf16),
            pltpu.VMEM((2, HALF, WIDTH), bf16),
            pltpu.VMEM((2, 8, HALF), jnp.float32),
            pltpu.VMEM((2, 8, HALF), jnp.float32),
            pltpu.VMEM((28, WIDTH), jnp.float32),
            pltpu.VMEM((2, TOKENS, PACK), bf16),
            pltpu.VMEM((TOKENS, PACK), bf16),
            pltpu.VMEM((CHUNKS, 32, PACK), bf16),
            pltpu.VMEM((CHUNKS, 32, PACK), bf16),
            pltpu.VMEM((CHUNKS, 32, PACK), bf16),
            pltpu.VMEM((CHUNKS, 32, PACK), bf16),
            pltpu.VMEM((CHUNKS, 16, PACK), bf16),
            pltpu.VMEM((2, 64, PACK), bf16),
            pltpu.VMEM((TOKENS, BACK), bf16),
            pltpu.VMEM((16, OWN, BACK), bf16),
            pltpu.SemaphoreType.DMA((COPY_SLOTS,)),
            pltpu.SemaphoreType.DMA((COPY_SLOTS,)),
            pltpu.SemaphoreType.DMA((LOCAL_SLOTS,)),
        ],
        compiler_params=pltpu.CompilerParams(
            collective_id=0, has_side_effects=True, vmem_limit_bytes=55 * 1024 * 1024
        ),
    )(
        tokens, upstream, norm_gain, gate_weight, up_weight, down_weight,
        gate_mask, up_mask, down_marks,
    )
    return pl.pallas_call(
        weight_kernel,
        out_shape=(
            jax.ShapeDtypeStruct((OWN, WIDTH), bf16),
            jax.ShapeDtypeStruct((OWN, WIDTH), bf16),
            jax.ShapeDtypeStruct((WIDTH, 2 * HALF), bf16),
            jax.ShapeDtypeStruct((WIDTH, 2 * HALF), bf16),
            jax.ShapeDtypeStruct((2 * HALF, WIDTH), bf16),
        ),
        in_specs=[in_vmem] * 8,
        out_specs=[in_vmem, in_vmem, anywhere, anywhere, anywhere],
        scratch_shapes=[
            pltpu.VMEM((2, WIDTH, HALF), bf16),
            pltpu.VMEM((2, WIDTH, HALF), bf16),
            pltpu.VMEM((2, HALF, WIDTH), bf16),
            pltpu.SemaphoreType.DMA((6,)),
        ],
        compiler_params=pltpu.CompilerParams(vmem_limit_bytes=24 * 1024 * 1024),
    )(sums_out, sums_in, xt, full, normed, gate_mask, up_mask, down_marks)


def solution(mesh):
    in_specs = (
        P("mp", "section"),
        P("mp", "section"),
        P("section"),
        P("section", "mp"),
        P("section", "mp"),
        P("mp", "section"),
        P("section", "mp"),
        P("section", "mp"),
        P("mp", "section"),
    )
    out_specs = (
        P("mp", "section"),
        P("mp", "section"),
        P("section", "mp"),
        P("section", "mp"),
        P("mp", "section"),
    )
    return jax.shard_map(
        on_device, mesh=mesh, in_specs=in_specs, out_specs=out_specs, check_vma=False
    )
```

```python
import jax
import jax.numpy as jnp
from jax import lax
from jax.experimental import pallas as pl
from jax.experimental.pallas import tpu as pltpu
from jax.sharding import PartitionSpec as P

D = 8192
BLOCK = 64
EPSILON = 1e-05

X_COUNT = 4
Z_COUNT = 8
OWN = 32
CHUNK = 128
CHUNKS = 4
TOKENS = 512
WIDTH = 512
HALF = 896
PACK = 3 * HALF + 128
BACK = 2 * WIDTH + 128

OFFSETS = ((0, 1), (-1, 2), (-2, 3), (-3, 4))
GROUP_ROW = {
    offset: CHUNK * chunk + 64 * place
    for chunk, pair in enumerate(OFFSETS)
    for place, offset in enumerate(pair)
}
LINE_FIRST = (False, False, True, False)
LINE_BUFFER = (0, 0, 0, 0)
DIRECT_SUM = (False, False, False, False)
DIRECT_BACK = (False, False, False, False)
COLUMNS = ((0, PACK // 2), (PACK // 2, PACK // 2))

ORDER = (
    (0, 1), (1, 0), (0, 2), (1, 1), (2, 0), (0, 3), (1, 2), (2, 1), (0, 4), (1, 3), (2, 2), (3, 1),
    (2, 3), (3, 3), (4, 1), (3, 0), (3, 2), (4, 3), (5, 1), (4, 2), (4, 0), (5, 3), (6, 1), (5, 2),
    (6, 3), (7, 1), (6, 2), (7, 3), (5, 0), (8, 1), (7, 2), (8, 3), (6, 0), (9, 1), (8, 2), (9, 3),
    (7, 0), (9, 2), (10, 1), (8, 0), (10, 3), (9, 0), (10, 2), (10, 0),
)
COPY_SLOTS = 120
SEND_SLOTS = 32
LOCAL_SLOTS = 8


def dot(left_side, right_side, left_dim, right_dim):
    return lax.dot_general(
        left_side,
        right_side,
        (((left_dim,), (right_dim,)), ((), ())),
        preferred_element_type=jnp.float32,
    )


def lanes(rows):
    return lax.broadcasted_iota(jnp.int32, (rows, 128), 1)


def split_sum(total):
    high = total.astype(jnp.bfloat16).astype(jnp.float32)
    return high, total - high


def pack_sums(first, second=None):
    lane = lanes(first.shape[0])
    high, low = split_sum(first)
    packed = jnp.where(lane == 0, high, jnp.where(lane == 1, low, 0.0))
    if second is not None:
        high, low = split_sum(second)
        packed = jnp.where(lane == 2, high, jnp.where(lane == 3, low, packed))
    return packed.astype(jnp.bfloat16)


def unpack_sum(packed, first_lane):
    lane = lanes(packed.shape[0])
    kept = (lane == first_lane) | (lane == first_lane + 1)
    return jnp.sum(
        jnp.where(kept, packed.astype(jnp.float32), 0.0), axis=1, keepdims=True
    )


def widen_mask(marks, rows, cols, first=0, marks_dim=1):
    marks_f = marks.astype(jnp.float32).astype(jnp.bfloat16)
    row = lax.broadcasted_iota(jnp.int32, (rows, cols), 0)
    col = lax.broadcasted_iota(jnp.int32, (rows, cols), 1) + first
    spread = jnp.where(row == (col >> 6), 1.0, 0.0).astype(jnp.bfloat16)
    return dot(marks_f, spread, marks_dim, 0)


def kernel(
    tokens, upstream, gain, gate_w, up_w, down_w, gate_m, up_m, down_m,
    layer_out, input_grad, xt, full, normed,
    gw, uw, dw, mg, mu, md, part, core_in, mid, near, far, summed, y_in, line_in,
    back, line_back, back_in, send, recv, local,
):
    section = lax.axis_index("section")
    mp = lax.axis_index("mp")
    core = lax.rem(section, 2)
    x = lax.rem(lax.div(section, 2), X_COUNT)
    y_hi = lax.div(section, 2 * X_COUNT)
    y_lo = lax.div(mp, Z_COUNT)
    z = lax.rem(mp, Z_COUNT)

    def section_of(y_at, x_at, core_at):
        return (y_at * X_COUNT + x_at) * 2 + core_at

    x_up, x_down = lax.rem(x + 1, X_COUNT), lax.rem(x + 3, X_COUNT)
    x_far = lax.rem(x + 2, X_COUNT)
    to_core = (section_of(y_hi, x, 1 - core), mp)
    to_x_up = (section_of(y_hi, x_up, core), mp)
    to_x_down = (section_of(y_hi, x_down, core), mp)
    to_x_far = (section_of(y_hi, x_far, core), mp)
    to_y = (section_of(1 - y_hi, x, core), mp)

    def mp_peer(line, offset):
        y_at = y_lo if line == 0 else 1 - y_lo
        return (section, y_at * Z_COUNT + lax.rem(z + offset + Z_COUNT, Z_COUNT))

    copies = []

    def remote(src, dst, device):
        slot = len(copies)
        if slot >= SEND_SLOTS:
            copies[slot - SEND_SLOTS].wait_send()
        copy = pltpu.make_async_remote_copy(
            src_ref=src,
            dst_ref=dst,
            send_sem=send.at[slot % SEND_SLOTS],
            recv_sem=recv.at[slot],
            device_id=device,
            device_id_type=pl.DeviceIdType.MESH,
        )
        copy.start()
        copies.append(copy)
        return copy

    local_count = [0]

    def nearby(src, dst):
        copy = pltpu.make_async_copy(src, dst, local.at[local_count[0]])
        local_count[0] += 1
        copy.start()
        return copy

    own_row = GROUP_ROW[0]
    own_rows = pl.ds(own_row, OWN)
    own_loads = [
        nearby(tokens, xt.at[own_rows, pl.ds(0, WIDTH)]),
        nearby(upstream, xt.at[own_rows, pl.ds(WIDTH, WIDTH)]),
    ]
    weight_loads = []
    for half in range(2):
        hidden = pl.ds(half * HALF, HALF)
        weight_loads.append(nearby(gate_w.at[:, hidden], gw.at[half]))
        weight_loads.append(nearby(up_w.at[:, hidden], uw.at[half]))
        weight_loads.append(nearby(down_w.at[hidden, :], dw.at[half]))

    to_line = mp_peer(1, 0)
    partners = [to_line]
    for offset in (1, -1, 2, -2):
        partners += [mp_peer(0, offset), mp_peer(1, offset)]
    partners += [to_core, to_x_up, to_x_down, to_y]
    if any(DIRECT_SUM + DIRECT_BACK):
        partners.append(to_x_far)
    barrier = pltpu.get_barrier_semaphore()
    for partner in partners:
        pl.semaphore_signal(
            barrier, inc=1, device_id=partner, device_id_type=pl.DeviceIdType.MESH
        )
    for load in own_loads:
        load.wait()
    pl.semaphore_wait(barrier, len(partners))

    def group(offset, first=0, rows=64):
        return xt.at[pl.ds(GROUP_ROW[offset] + first, rows), :]

    def send_own(line, offset):
        return remote(
            group(0, 0, OWN), group(-offset, line * OWN, OWN), mp_peer(line, offset)
        )

    arriving = {0: [send_own(1, 0)]}
    for offset in (1, -1, 2, -2):
        arriving[-offset] = [send_own(0, offset), send_own(1, offset)]

    gain_f = gain[...].astype(jnp.float32).reshape(1, WIDTH)
    for half in range(2):
        mg[half] = widen_mask(gate_m[...], 28, HALF, half * HALF)
        mu[half] = widen_mask(up_m[...], 28, HALF, half * HALF)
    md[...] = widen_mask(down_m[...], 8, WIDTH, 0, 0)

    for load in weight_loads:
        load.wait()

    for half in range(2):

        def mask_rows(block, carry):
            rows = pl.ds(pl.multiple_of(block * BLOCK, BLOCK), BLOCK)
            at = pl.ds(block, 1)
            gw[half, rows, :] = (gw[half, rows, :].astype(jnp.float32) * mg[half, at, :]).astype(
                jnp.bfloat16
            )
            uw[half, rows, :] = (uw[half, rows, :].astype(jnp.float32) * mu[half, at, :]).astype(
                jnp.bfloat16
            )
            return carry

        def mask_down_rows(block, carry):
            rows = pl.ds(pl.multiple_of(block * BLOCK, BLOCK), BLOCK)
            at = pl.ds(block + half * (HALF // BLOCK), 1)
            dw[half, rows, :] = (dw[half, rows, :].astype(jnp.float32) * md[at, :]).astype(
                jnp.bfloat16
            )
            return carry

        lax.fori_loop(0, WIDTH // BLOCK, mask_rows, 0)
        lax.fori_loop(0, HALF // BLOCK, mask_down_rows, 0)

    def token_step(step):
        for offset in (0, 1, -1) if step == 1 else (step, -step) if step < 4 else (4,):
            for copy in arriving[offset]:
                copy.wait_recv()
        if step == 1:
            arriving[-3] = [remote(group(-1), group(-3), mp_peer(0, 2))]
            arriving[3] = [remote(group(1), group(3), mp_peer(0, -2))]
        elif step == 2:
            arriving[4] = [
                remote(group(-2, 0, OWN), group(4, 0, OWN), mp_peer(0, 2)),
                remote(group(2, OWN, OWN), group(4, OWN, OWN), mp_peer(0, -2)),
            ]

    pending = {}

    def row_of(chunk, x_at, y_at=0):
        if LINE_FIRST[chunk]:
            return pl.multiple_of(chunk * CHUNK + y_at * 64 + x_at * 16, 16)
        return pl.multiple_of(chunk * CHUNK + x_at * 32 + y_at * 16, 16)

    def line_rows(chunk, y_at):
        return pl.ds(pl.multiple_of(chunk * CHUNK + y_at * 64, 64), 64)

    def products(chunk):
        rows = pl.ds(chunk * CHUNK, CHUNK)
        values = xt[rows, 0:WIDTH].astype(jnp.float32)
        gained = (values * gain_f).astype(jnp.bfloat16)
        back_values = xt[rows, WIDTH : 2 * WIDTH]
        sums = pack_sums(jnp.sum(values * values, axis=1, keepdims=True))
        for turn in range(2):
            half = 1 - core if turn == 0 else core
            part[half, rows, 0:HALF] = dot(gained, gw[half], 1, 0).astype(jnp.bfloat16)
            part[half, rows, HALF : 2 * HALF] = dot(gained, uw[half], 1, 0).astype(jnp.bfloat16)
            part[half, rows, 2 * HALF : 3 * HALF] = dot(back_values, dw[half], 1, 1).astype(
                jnp.bfloat16
            )
            part[half, rows, 3 * HALF :] = sums
            if turn == 0:
                pending["core", chunk] = remote(
                    part.at[half, rows, :], core_in.at[rows, :], to_core
                )

    def store_sum(ref, total_fn):
        ref[..., 0 : 3 * HALF] = total_fn(slice(0, 3 * HALF)).astype(jnp.bfloat16)
        ref[..., 3 * HALF :] = pack_sums(unpack_sum(total_fn(slice(3 * HALF, PACK)), 0))

    def add_pieces(first_row, count, source, source_row):
        def add_rows(piece, carry):
            rows = pl.ds(pl.multiple_of(first_row + piece * 16, 16), 16)
            source_rows = pl.ds(pl.multiple_of(source_row + piece * 16, 16), 16)
            store_sum(
                part.at[core, rows, :],
                lambda cols: part[core, rows, cols].astype(jnp.float32)
                + source[source_rows, cols].astype(jnp.float32),
            )
            return carry

        lax.fori_loop(0, count, add_rows, 0)

    def x_part(chunk, x_at):
        if LINE_FIRST[chunk]:
            return pl.ds(row_of(chunk, x_at, y_hi), 16)
        return pl.ds(row_of(chunk, x_at), 32)

    def part_size(chunk):
        return 16 if LINE_FIRST[chunk] else 32

    def start_ring(chunk):
        rows = pl.ds(0, part_size(chunk))
        if DIRECT_SUM[chunk]:
            pending["near", chunk] = [
                remote(
                    part.at[core, x_part(chunk, x_at), :], target.at[chunk, rows, :], device
                )
                for x_at, target, device in (
                    (x_up, near, to_x_up), (x_down, far, to_x_down), (x_far, mid, to_x_far)
                )
            ]
            pending["far", chunk] = []
            return

        def columns(x_at, turn, target, device):
            cols = pl.ds(*COLUMNS[turn])
            return remote(
                part.at[core, x_part(chunk, x_at), cols], target.at[chunk, rows, cols], device
            )

        pending["mid", chunk] = (
            columns(x_far, 0, mid, to_x_up), columns(x_far, 1, mid, to_x_down)
        )
        pending["near", chunk] = (
            columns(x_up, 1, near, to_x_up), columns(x_down, 0, near, to_x_down)
        )

    def turn_ring(chunk):
        if DIRECT_SUM[chunk]:
            return
        here = pl.ds(0, part_size(chunk))
        sent = []
        for turn, (x_at, device) in enumerate(((x_up, to_x_up), (x_down, to_x_down))):
            pending["mid", chunk][turn].wait_recv()
            rows = x_part(chunk, x_at)
            first, width = COLUMNS[turn]
            plain = width if turn == 0 else width - 128
            cols = slice(first, first + plain)
            part[core, rows, cols] = (
                part[core, rows, cols].astype(jnp.float32)
                + mid[chunk, here, cols].astype(jnp.float32)
            ).astype(jnp.bfloat16)
            if turn == 1:
                cols = slice(3 * HALF, PACK)
                part[core, rows, cols] = pack_sums(
                    unpack_sum(part[core, rows, cols], 0) + unpack_sum(mid[chunk, here, cols], 0)
                )
            cols = pl.ds(first, width)
            sent.append(remote(part.at[core, rows, cols], far.at[chunk, here, cols], device))
        pending["far", chunk] = sent

    def ring_total(chunk, cols):
        here = slice(0, part_size(chunk))
        total = (
            part[core, x_part(chunk, x), cols].astype(jnp.float32)
            + near[chunk, here, cols].astype(jnp.float32)
            + far[chunk, here, cols].astype(jnp.float32)
        )
        if DIRECT_SUM[chunk]:
            total = total + mid[chunk, here, cols].astype(jnp.float32)
        return total

    def wait_ring(chunk):
        for copy in (*pending["near", chunk], *pending["far", chunk]):
            copy.wait_recv()

    def add_cores(chunk):
        pending["core", chunk].wait_recv()
        add_pieces(chunk * CHUNK, CHUNK // 16, core_in, chunk * CHUNK)
        if LINE_FIRST[chunk]:
            pending["line", chunk] = remote(
                part.at[core, line_rows(chunk, 1 - y_hi), :],
                line_in.at[LINE_BUFFER[chunk]],
                to_y,
            )
        else:
            start_ring(chunk)

    def third(chunk):
        if LINE_FIRST[chunk]:
            pending["line", chunk].wait_recv()
            add_pieces(
                chunk * CHUNK + y_hi * 64, 4, line_in.at[LINE_BUFFER[chunk]], 0
            )
            start_ring(chunk)
        else:
            turn_ring(chunk)

    def fourth(chunk):
        if LINE_FIRST[chunk]:
            turn_ring(chunk)
            return
        wait_ring(chunk)
        store_sum(summed.at[chunk], lambda cols: ring_total(chunk, cols))
        other = pl.ds(pl.multiple_of((1 - y_hi) * 16, 16), 16)
        pending["y", chunk] = remote(summed.at[chunk, other, :], y_in.at[chunk], to_y)

    def activate(chunk):
        if LINE_FIRST[chunk]:
            wait_ring(chunk)
        else:
            pending["y", chunk].wait_recv()
        kept = pl.ds(pl.multiple_of(y_hi * 16, 16), 16)

        def total(first, last):
            if LINE_FIRST[chunk]:
                return ring_total(chunk, slice(first, last))
            return summed[chunk, kept, first:last].astype(jnp.float32) + y_in[
                chunk, :, first:last
            ].astype(jnp.float32)

        squares = unpack_sum(total(3 * HALF, PACK), 0)
        inv_rms = lax.rsqrt(squares / D + EPSILON)
        gate_pre = total(0, HALF) * inv_rms
        up_pre = total(HALF, 2 * HALF) * inv_rms
        grad_act = total(2 * HALF, 3 * HALF)
        sigmoid_gate = jax.nn.sigmoid(gate_pre)
        gated = gate_pre * sigmoid_gate
        grad_gate = (
            grad_act * up_pre * sigmoid_gate * (1.0 + gate_pre * (1.0 - sigmoid_gate))
        ).astype(jnp.bfloat16)
        grad_up = (grad_act * gated).astype(jnp.bfloat16)
        inner = jnp.sum(
            grad_gate.astype(jnp.float32) * gate_pre + grad_up.astype(jnp.float32) * up_pre,
            axis=1,
            keepdims=True,
        )
        rows = pl.ds(row_of(chunk, x, y_hi), 16)
        full[core, rows, 0:HALF] = (gated * up_pre).astype(jnp.bfloat16)
        full[core, rows, HALF : 2 * HALF] = grad_gate
        full[core, rows, 2 * HALF : 3 * HALF] = grad_up
        full[core, rows, 3 * HALF :] = pack_sums(inv_rms, inner)
        piece = full.at[core, rows, :]
        pending["y_back", chunk] = [same_place(piece, to_y)]
        pending["x_back", chunk] = [same_place(piece, to_x_up), same_place(piece, to_x_down)]
        pending["x_far", chunk] = []
        if DIRECT_BACK[chunk]:
            pending["x_far", chunk].append(same_place(piece, to_x_far))
        pending["core_back", chunk] = []

    def same_place(piece, device):
        return remote(piece, piece, device)

    def full_rows(chunk, x_at, y_at, rows=16, turn=None):
        cols = pl.ds(0, PACK) if turn is None else pl.ds(*COLUMNS[turn])
        return full.at[core, pl.ds(row_of(chunk, x_at, y_at), rows), cols]

    def to_other_core(chunk, piece):
        pending["core_back", chunk].append(same_place(piece, to_core))

    def wait_all(key, chunk):
        for copy in pending[key, chunk]:
            copy.wait_recv()

    def sixth(chunk):
        if LINE_FIRST[chunk]:
            wait_all("x_back", chunk)
            if not DIRECT_BACK[chunk]:
                pending["x_far", chunk] = (
                    same_place(full_rows(chunk, x_down, y_hi, 16, 0), to_x_up),
                    same_place(full_rows(chunk, x_up, y_hi, 16, 1), to_x_down),
                )
            for x_at in (x_down, x_up):
                pending["y_back", chunk].append(
                    same_place(full_rows(chunk, x_at, y_hi), to_y)
                )
        else:
            wait_all("y_back", chunk)
            piece = full_rows(chunk, x, 1 - y_hi)
            pending["x_back", chunk] += [
                same_place(piece, to_x_up), same_place(piece, to_x_down)
            ]
            if DIRECT_BACK[chunk]:
                pending["x_far", chunk].append(same_place(piece, to_x_far))
            to_other_core(chunk, full_rows(chunk, x, 0, 32))

    def seventh(chunk):
        if LINE_FIRST[chunk]:
            wait_all("x_far", chunk)
            pending["y_back", chunk].append(
                same_place(full_rows(chunk, x_far, y_hi), to_y)
            )
            to_other_core(chunk, full.at[core, line_rows(chunk, y_hi), :])
        else:
            wait_all("x_back", chunk)
            if not DIRECT_BACK[chunk]:
                pending["x_far", chunk] = (
                    same_place(full_rows(chunk, x_down, 0, 32, 0), to_x_up),
                    same_place(full_rows(chunk, x_up, 0, 32, 1), to_x_down),
                )
            to_other_core(chunk, full_rows(chunk, x_down, 0, 32))
            to_other_core(chunk, full_rows(chunk, x_up, 0, 32))

    def eighth(chunk):
        if LINE_FIRST[chunk]:
            wait_all("y_back", chunk)
            to_other_core(chunk, full.at[core, line_rows(chunk, 1 - y_hi), :])
        else:
            wait_all("x_far", chunk)
            to_other_core(chunk, full_rows(chunk, x_far, 0, 32))

    def finish(chunk):
        for copy in pending["core_back", chunk]:
            copy.wait_recv()
        rows = pl.ds(chunk * CHUNK, CHUNK)
        down_sum = dot(full[0, rows, 0:HALF], dw[0], 1, 0) + dot(
            full[1, rows, 0:HALF], dw[1], 1, 0
        )
        back[rows, 0:WIDTH] = down_sum.astype(jnp.bfloat16)
        grad_sum = (
            dot(full[0, rows, HALF : 2 * HALF], gw[0], 1, 1)
            + dot(full[1, rows, HALF : 2 * HALF], gw[1], 1, 1)
            + dot(full[0, rows, 2 * HALF : 3 * HALF], uw[0], 1, 1)
            + dot(full[1, rows, 2 * HALF : 3 * HALF], uw[1], 1, 1)
        )
        back[rows, WIDTH : 2 * WIDTH] = grad_sum.astype(jnp.bfloat16)
        sums = full[0, rows, 3 * HALF :]
        back[rows, 2 * WIDTH :] = pack_sums(
            unpack_sum(sums, 2) + unpack_sum(full[1, rows, 3 * HALF :], 2)
        )
        pending["line_back", chunk] = [
            remote(
                back.at[pl.ds(chunk * CHUNK + place * 64 + OWN, OWN), :],
                line_back.at[chunk, pl.ds(place * OWN, OWN), :],
                to_line,
            )
            for place in range(2)
        ]
        inv_rms = unpack_sum(sums, 0)
        normed[rows, :] = (xt[rows, 0:WIDTH].astype(jnp.float32) * inv_rms * gain_f).astype(
            jnp.bfloat16
        )

    def add_back(chunk):
        wait_all("line_back", chunk)
        for place, offset in enumerate(OFFSETS[chunk]):
            rows = pl.ds(chunk * CHUNK + place * 64, OWN)
            here = pl.ds(place * OWN, OWN)
            plain = slice(0, 2 * WIDTH)
            back[rows, plain] = (
                back[rows, plain].astype(jnp.float32)
                + line_back[chunk, here, plain].astype(jnp.float32)
            ).astype(jnp.bfloat16)
            back[rows, 2 * WIDTH :] = pack_sums(
                unpack_sum(back[rows, 2 * WIDTH :], 0)
                + unpack_sum(line_back[chunk, here, 2 * WIDTH :], 0)
            )
            if offset:
                pending["back", offset] = remote(
                    back.at[rows, :], back_in.at[offset % Z_COUNT], mp_peer(0, offset)
                )

    stages = (
        token_step, products, add_cores, third, fourth, activate, sixth, seventh, eighth, finish,
        add_back,
    )
    for stage, which in ORDER:
        stages[stage](which)

    total = back[own_rows, :].astype(jnp.float32)
    for offset in (1, -1, 2, -2, 3, -3, 4):
        pending["back", offset].wait_recv()
        total = total + back_in[offset % Z_COUNT].astype(jnp.float32)
    inputs_f = xt[own_rows, 0:WIDTH].astype(jnp.float32)
    layer_out[...] = (inputs_f + total[:, 0:WIDTH]).astype(jnp.bfloat16)
    inner_mean = unpack_sum(total[:, 2 * WIDTH :], 0) / D
    inv_rms = unpack_sum(full[0, own_rows, 3 * HALF :], 0)
    grad_scaled = total[:, WIDTH : 2 * WIDTH] * gain_f
    input_grad[...] = (
        xt[own_rows, WIDTH : 2 * WIDTH].astype(jnp.float32)
        + inv_rms * (grad_scaled - inputs_f * inv_rms * inner_mean)
    ).astype(jnp.bfloat16)

    for copy in copies[-SEND_SLOTS:]:
        copy.wait_send()


def weight_kernel(
    sums_out, sums_in, xt, full, normed, gate_m, up_m, down_m,
    layer_out, input_grad, gate_grad, up_grad, down_grad,
    gate_stage, up_stage, down_stage, local,
):
    layer_out[...] = sums_out[...]
    input_grad[...] = sums_in[...]
    marks_d = widen_mask(down_m[...], 8, WIDTH, 0, 0)
    upstream_full = xt[:, WIDTH : 2 * WIDTH]
    stores = []

    def store(src, dst):
        copy = pltpu.make_async_copy(src, dst, local.at[len(stores)])
        copy.start()
        stores.append(copy)

    for half in range(2):
        hidden = pl.ds(half * HALF, HALF)
        grads = dot(full[half, :, 0:HALF], upstream_full, 0, 0)
        for block in range(HALF // BLOCK):
            rows = slice(block * BLOCK, (block + 1) * BLOCK)
            mark = half * (HALF // BLOCK) + block
            down_stage[half, rows, :] = (
                grads[rows, :] * marks_d[mark : mark + 1, :]
            ).astype(jnp.bfloat16)
        store(down_stage.at[half], down_grad.at[hidden, :])
        for which, stage, given, target in (
            (0, gate_stage, gate_m, gate_grad), (1, up_stage, up_m, up_grad)
        ):
            first = (1 + which) * HALF
            marks = widen_mask(given[...], 28, HALF, half * HALF)
            grads = dot(normed[...], full[half, :, first : first + HALF], 0, 0)
            for block in range(WIDTH // BLOCK):
                rows = slice(block * BLOCK, (block + 1) * BLOCK)
                stage[half, rows, :] = (grads[rows, :] * marks[block : block + 1, :]).astype(
                    jnp.bfloat16
                )
            store(stage.at[half], target.at[:, hidden])
    for copy in stores:
        copy.wait()


def on_device(
    tokens, upstream, norm_gain, gate_weight, up_weight, down_weight, gate_mask, up_mask, down_mask
):
    in_vmem = pl.BlockSpec(memory_space=pltpu.VMEM)
    anywhere = pl.BlockSpec(memory_space=pl.ANY)
    bf16 = jnp.bfloat16
    down_marks = down_mask.T
    sums_out, sums_in, xt, full, normed = pl.pallas_call(
        kernel,
        out_shape=(
            pltpu.VMEM((OWN, WIDTH), bf16),
            pltpu.VMEM((OWN, WIDTH), bf16),
            pltpu.VMEM((TOKENS, 2 * WIDTH), bf16),
            pltpu.VMEM((2, TOKENS, PACK), bf16),
            pltpu.VMEM((TOKENS, WIDTH), bf16),
        ),
        in_specs=[anywhere, anywhere, in_vmem] + [anywhere] * 3 + [in_vmem] * 3,
        out_specs=[in_vmem] * 5,
        scratch_shapes=[
            pltpu.VMEM((2, WIDTH, HALF), bf16),
            pltpu.VMEM((2, WIDTH, HALF), bf16),
            pltpu.VMEM((2, HALF, WIDTH), bf16),
            pltpu.VMEM((2, 8, HALF), jnp.float32),
            pltpu.VMEM((2, 8, HALF), jnp.float32),
            pltpu.VMEM((28, WIDTH), jnp.float32),
            pltpu.VMEM((2, TOKENS, PACK), bf16),
            pltpu.VMEM((TOKENS, PACK), bf16),
            pltpu.VMEM((CHUNKS, 32, PACK), bf16),
            pltpu.VMEM((CHUNKS, 32, PACK), bf16),
            pltpu.VMEM((CHUNKS, 32, PACK), bf16),
            pltpu.VMEM((CHUNKS, 32, PACK), bf16),
            pltpu.VMEM((CHUNKS, 16, PACK), bf16),
            pltpu.VMEM((1, 64, PACK), bf16),
            pltpu.VMEM((TOKENS, BACK), bf16),
            pltpu.VMEM((CHUNKS, 64, BACK), bf16),
            pltpu.VMEM((Z_COUNT, OWN, BACK), bf16),
            pltpu.SemaphoreType.DMA((SEND_SLOTS,)),
            pltpu.SemaphoreType.DMA((COPY_SLOTS,)),
            pltpu.SemaphoreType.DMA((LOCAL_SLOTS,)),
        ],
        compiler_params=pltpu.CompilerParams(
            collective_id=0, has_side_effects=True, vmem_limit_bytes=55 * 1024 * 1024
        ),
    )(
        tokens, upstream, norm_gain, gate_weight, up_weight, down_weight,
        gate_mask, up_mask, down_marks,
    )
    return pl.pallas_call(
        weight_kernel,
        out_shape=(
            jax.ShapeDtypeStruct((OWN, WIDTH), bf16),
            jax.ShapeDtypeStruct((OWN, WIDTH), bf16),
            jax.ShapeDtypeStruct((WIDTH, 2 * HALF), bf16),
            jax.ShapeDtypeStruct((WIDTH, 2 * HALF), bf16),
            jax.ShapeDtypeStruct((2 * HALF, WIDTH), bf16),
        ),
        in_specs=[in_vmem] * 8,
        out_specs=[in_vmem, in_vmem, anywhere, anywhere, anywhere],
        scratch_shapes=[
            pltpu.VMEM((2, WIDTH, HALF), bf16),
            pltpu.VMEM((2, WIDTH, HALF), bf16),
            pltpu.VMEM((2, HALF, WIDTH), bf16),
            pltpu.SemaphoreType.DMA((6,)),
        ],
        compiler_params=pltpu.CompilerParams(vmem_limit_bytes=24 * 1024 * 1024),
    )(sums_out, sums_in, xt, full, normed, gate_mask, up_mask, down_marks)


def solution(mesh):
    in_specs = (
        P("mp", "section"),
        P("mp", "section"),
        P("section"),
        P("section", "mp"),
        P("section", "mp"),
        P("mp", "section"),
        P("section", "mp"),
        P("section", "mp"),
        P("mp", "section"),
    )
    out_specs = (
        P("mp", "section"),
        P("mp", "section"),
        P("section", "mp"),
        P("section", "mp"),
        P("mp", "section"),
    )
    return jax.shard_map(
        on_device, mesh=mesh, in_specs=in_specs, out_specs=out_specs, check_vma=False
    )
```

```python
import jax
import jax.numpy as jnp
from jax import lax
from jax.experimental import pallas as pl
from jax.experimental.pallas import tpu as pltpu
from jax.sharding import PartitionSpec as P

D = 8192
BLOCK = 64
EPSILON = 1e-05

X_COUNT = 4
Z_COUNT = 8
OWN = 32
CHUNK = 128
CHUNKS = 4
TOKENS = 512
WIDTH = 512
HALF = 896
PACK = 3 * HALF + 128
BACK = 2 * WIDTH + 128

OFFSETS = ((0, 1), (-1, 2), (-2, 3), (-3, 4))
GROUP_ROW = {
    offset: CHUNK * chunk + 64 * place
    for chunk, pair in enumerate(OFFSETS)
    for place, offset in enumerate(pair)
}
LINE_FIRST = (False, False, True, False)
LINE_BUFFER = (0, 0, 0, 0)
DIRECT_SUM = (False, False, False, False)
DIRECT_BACK = (False, False, False, False)
COLUMNS = ((0, PACK // 2), (PACK // 2, PACK // 2))

ORDER = (
    (0, 1), (1, 0), (0, 2), (1, 1), (2, 0), (0, 3), (1, 2), (2, 1), (0, 4), (1, 3), (2, 2), (3, 1),
    (2, 3), (3, 3), (4, 1), (3, 0), (3, 2), (4, 3), (5, 1), (4, 2), (4, 0), (5, 3), (6, 1), (5, 2),
    (6, 3), (7, 1), (6, 2), (7, 3), (5, 0), (8, 1), (7, 2), (8, 3), (6, 0), (9, 1), (8, 2), (9, 3),
    (7, 0), (9, 2), (10, 1), (8, 0), (10, 3), (9, 0), (10, 2), (10, 0),
)
COPY_SLOTS = 108
SEND_SLOTS = 24
LOCAL_SLOTS = 8


def dot(left_side, right_side, left_dim, right_dim):
    return lax.dot_general(
        left_side,
        right_side,
        (((left_dim,), (right_dim,)), ((), ())),
        preferred_element_type=jnp.float32,
    )


def lanes(rows):
    return lax.broadcasted_iota(jnp.int32, (rows, 128), 1)


def split_sum(total):
    high = total.astype(jnp.bfloat16).astype(jnp.float32)
    return high, total - high


def pack_sums(first, second=None):
    lane = lanes(first.shape[0])
    high, low = split_sum(first)
    packed = jnp.where(lane == 0, high, jnp.where(lane == 1, low, 0.0))
    if second is not None:
        high, low = split_sum(second)
        packed = jnp.where(lane == 2, high, jnp.where(lane == 3, low, packed))
    return packed.astype(jnp.bfloat16)


def unpack_sum(packed, first_lane):
    lane = lanes(packed.shape[0])
    kept = (lane == first_lane) | (lane == first_lane + 1)
    return jnp.sum(
        jnp.where(kept, packed.astype(jnp.float32), 0.0), axis=1, keepdims=True
    )


def widen_mask(marks, rows, cols, first=0, marks_dim=1):
    marks_f = marks.astype(jnp.float32).astype(jnp.bfloat16)
    row = lax.broadcasted_iota(jnp.int32, (rows, cols), 0)
    col = lax.broadcasted_iota(jnp.int32, (rows, cols), 1) + first
    spread = jnp.where(row == (col >> 6), 1.0, 0.0).astype(jnp.bfloat16)
    return dot(marks_f, spread, marks_dim, 0)


def kernel(
    tokens, upstream, gain, gate_w, up_w, down_w, gate_m, up_m, down_m,
    layer_out, input_grad, xt, full, normed,
    gw, uw, dw, mg, mu, md, part, core_in, mid, near, far, summed, y_in, line_in,
    back, line_back, back_in, send, recv, local,
):
    section = lax.axis_index("section")
    mp = lax.axis_index("mp")
    core = lax.rem(section, 2)
    x = lax.rem(lax.div(section, 2), X_COUNT)
    y_hi = lax.div(section, 2 * X_COUNT)
    y_lo = lax.div(mp, Z_COUNT)
    z = lax.rem(mp, Z_COUNT)

    def section_of(y_at, x_at, core_at):
        return (y_at * X_COUNT + x_at) * 2 + core_at

    x_up, x_down = lax.rem(x + 1, X_COUNT), lax.rem(x + 3, X_COUNT)
    x_far = lax.rem(x + 2, X_COUNT)
    to_core = (section_of(y_hi, x, 1 - core), mp)
    to_x_up = (section_of(y_hi, x_up, core), mp)
    to_x_down = (section_of(y_hi, x_down, core), mp)
    to_x_far = (section_of(y_hi, x_far, core), mp)
    to_y = (section_of(1 - y_hi, x, core), mp)

    def mp_peer(line, offset):
        y_at = y_lo if line == 0 else 1 - y_lo
        return (section, y_at * Z_COUNT + lax.rem(z + offset + Z_COUNT, Z_COUNT))

    copies = []

    def remote(src, dst, device):
        slot = len(copies)
        if slot >= SEND_SLOTS:
            copies[slot - SEND_SLOTS].wait_send()
        copy = pltpu.make_async_remote_copy(
            src_ref=src,
            dst_ref=dst,
            send_sem=send.at[slot % SEND_SLOTS],
            recv_sem=recv.at[slot],
            device_id=device,
            device_id_type=pl.DeviceIdType.MESH,
        )
        copy.start()
        copies.append(copy)
        return copy

    local_count = [0]

    def nearby(src, dst):
        copy = pltpu.make_async_copy(src, dst, local.at[local_count[0]])
        local_count[0] += 1
        copy.start()
        return copy

    own_row = GROUP_ROW[0]
    own_rows = pl.ds(own_row, OWN)
    own_loads = [
        nearby(tokens, xt.at[own_rows, pl.ds(0, WIDTH)]),
        nearby(upstream, xt.at[own_rows, pl.ds(WIDTH, WIDTH)]),
    ]
    weight_loads = []
    for half in range(2):
        hidden = pl.ds(half * HALF, HALF)
        weight_loads.append(nearby(gate_w.at[:, hidden], gw.at[half]))
        weight_loads.append(nearby(up_w.at[:, hidden], uw.at[half]))
        weight_loads.append(nearby(down_w.at[hidden, :], dw.at[half]))

    to_line = mp_peer(1, 0)
    partners = [to_line]
    for offset in (1, -1, 2, -2):
        partners += [mp_peer(0, offset), mp_peer(1, offset)]
    partners += [to_core, to_x_up, to_x_down, to_y]
    if any(DIRECT_SUM + DIRECT_BACK):
        partners.append(to_x_far)
    barrier = pltpu.get_barrier_semaphore()
    for partner in partners:
        pl.semaphore_signal(
            barrier, inc=1, device_id=partner, device_id_type=pl.DeviceIdType.MESH
        )
    for load in own_loads:
        load.wait()
    pl.semaphore_wait(barrier, len(partners))

    def group(offset, first=0, rows=64):
        return xt.at[pl.ds(GROUP_ROW[offset] + first, rows), :]

    def send_own(line, offset):
        return remote(
            group(0, 0, OWN), group(-offset, line * OWN, OWN), mp_peer(line, offset)
        )

    arriving = {0: [send_own(1, 0)]}
    for offset in (1, -1, 2, -2):
        arriving[-offset] = [send_own(0, offset), send_own(1, offset)]

    gain_f = gain[...].astype(jnp.float32).reshape(1, WIDTH)
    for half in range(2):
        mg[half] = widen_mask(gate_m[...], 28, HALF, half * HALF)
        mu[half] = widen_mask(up_m[...], 28, HALF, half * HALF)
    md[...] = widen_mask(down_m[...], 8, WIDTH, 0, 0)

    for load in weight_loads:
        load.wait()

    for half in range(2):

        def mask_rows(block, carry):
            rows = pl.ds(pl.multiple_of(block * BLOCK, BLOCK), BLOCK)
            at = pl.ds(block, 1)
            gw[half, rows, :] = (gw[half, rows, :].astype(jnp.float32) * mg[half, at, :]).astype(
                jnp.bfloat16
            )
            uw[half, rows, :] = (uw[half, rows, :].astype(jnp.float32) * mu[half, at, :]).astype(
                jnp.bfloat16
            )
            return carry

        def mask_down_rows(block, carry):
            rows = pl.ds(pl.multiple_of(block * BLOCK, BLOCK), BLOCK)
            at = pl.ds(block + half * (HALF // BLOCK), 1)
            dw[half, rows, :] = (dw[half, rows, :].astype(jnp.float32) * md[at, :]).astype(
                jnp.bfloat16
            )
            return carry

        lax.fori_loop(0, WIDTH // BLOCK, mask_rows, 0)
        lax.fori_loop(0, HALF // BLOCK, mask_down_rows, 0)

    def token_step(step):
        for offset in (0, 1, -1) if step == 1 else (step, -step) if step < 4 else (4,):
            for copy in arriving[offset]:
                copy.wait_recv()
        if step == 1:
            arriving[-3] = [remote(group(-1), group(-3), mp_peer(0, 2))]
            arriving[3] = [remote(group(1), group(3), mp_peer(0, -2))]
        elif step == 2:
            arriving[4] = [
                remote(group(-2, 0, OWN), group(4, 0, OWN), mp_peer(0, 2)),
                remote(group(2, OWN, OWN), group(4, OWN, OWN), mp_peer(0, -2)),
            ]

    pending = {}

    def row_of(chunk, x_at, y_at=0):
        if LINE_FIRST[chunk]:
            return pl.multiple_of(chunk * CHUNK + y_at * 64 + x_at * 16, 16)
        return pl.multiple_of(chunk * CHUNK + x_at * 32 + y_at * 16, 16)

    def line_rows(chunk, y_at):
        return pl.ds(pl.multiple_of(chunk * CHUNK + y_at * 64, 64), 64)

    def products(chunk):
        rows = pl.ds(chunk * CHUNK, CHUNK)
        values = xt[rows, 0:WIDTH].astype(jnp.float32)
        gained = (values * gain_f).astype(jnp.bfloat16)
        back_values = xt[rows, WIDTH : 2 * WIDTH]
        sums = pack_sums(jnp.sum(values * values, axis=1, keepdims=True))
        for turn in range(2):
            half = 1 - core if turn == 0 else core
            part[half, rows, 0:HALF] = dot(gained, gw[half], 1, 0).astype(jnp.bfloat16)
            part[half, rows, HALF : 2 * HALF] = dot(gained, uw[half], 1, 0).astype(jnp.bfloat16)
            part[half, rows, 2 * HALF : 3 * HALF] = dot(back_values, dw[half], 1, 1).astype(
                jnp.bfloat16
            )
            part[half, rows, 3 * HALF :] = sums
            if turn == 0:
                pending["core", chunk] = remote(
                    part.at[half, rows, :], core_in.at[rows, :], to_core
                )

    def store_sum(ref, total_fn):
        ref[..., 0 : 3 * HALF] = total_fn(slice(0, 3 * HALF)).astype(jnp.bfloat16)
        ref[..., 3 * HALF :] = pack_sums(unpack_sum(total_fn(slice(3 * HALF, PACK)), 0))

    def add_pieces(first_row, count, source, source_row):
        def add_rows(piece, carry):
            rows = pl.ds(pl.multiple_of(first_row + piece * 16, 16), 16)
            source_rows = pl.ds(pl.multiple_of(source_row + piece * 16, 16), 16)
            plain = slice(0, 3 * HALF)
            part[core, rows, plain] = part[core, rows, plain] + source[source_rows, plain]
            sums = slice(3 * HALF, PACK)
            part[core, rows, sums] = pack_sums(
                unpack_sum(part[core, rows, sums], 0) + unpack_sum(source[source_rows, sums], 0)
            )
            return carry

        lax.fori_loop(0, count, add_rows, 0)

    def x_part(chunk, x_at):
        if LINE_FIRST[chunk]:
            return pl.ds(row_of(chunk, x_at, y_hi), 16)
        return pl.ds(row_of(chunk, x_at), 32)

    def part_size(chunk):
        return 16 if LINE_FIRST[chunk] else 32

    def start_ring(chunk):
        rows = pl.ds(0, part_size(chunk))
        if DIRECT_SUM[chunk]:
            pending["near", chunk] = [
                remote(
                    part.at[core, x_part(chunk, x_at), :], target.at[chunk, rows, :], device
                )
                for x_at, target, device in (
                    (x_up, near, to_x_up), (x_down, far, to_x_down), (x_far, mid, to_x_far)
                )
            ]
            pending["far", chunk] = []
            return

        def columns(x_at, turn, target, device):
            cols = pl.ds(*COLUMNS[turn])
            return remote(
                part.at[core, x_part(chunk, x_at), cols], target.at[chunk, rows, cols], device
            )

        pending["mid", chunk] = (
            columns(x_far, 0, mid, to_x_up), columns(x_far, 1, mid, to_x_down)
        )
        pending["near", chunk] = (
            columns(x_up, 1, near, to_x_up), columns(x_down, 0, near, to_x_down)
        )

    def turn_ring(chunk):
        if DIRECT_SUM[chunk]:
            return
        here = pl.ds(0, part_size(chunk))
        sent = []
        for turn, (x_at, device) in enumerate(((x_up, to_x_up), (x_down, to_x_down))):
            pending["mid", chunk][turn].wait_recv()
            rows = x_part(chunk, x_at)
            first, width = COLUMNS[turn]
            plain = width if turn == 0 else width - 128
            cols = slice(first, first + plain)
            part[core, rows, cols] = part[core, rows, cols] + mid[chunk, here, cols]
            if turn == 1:
                cols = slice(3 * HALF, PACK)
                part[core, rows, cols] = pack_sums(
                    unpack_sum(part[core, rows, cols], 0) + unpack_sum(mid[chunk, here, cols], 0)
                )
            cols = pl.ds(first, width)
            sent.append(remote(part.at[core, rows, cols], far.at[chunk, here, cols], device))
        pending["far", chunk] = sent

    def ring_total(chunk, cols):
        here = slice(0, part_size(chunk))
        total = (
            part[core, x_part(chunk, x), cols].astype(jnp.float32)
            + near[chunk, here, cols].astype(jnp.float32)
            + far[chunk, here, cols].astype(jnp.float32)
        )
        if DIRECT_SUM[chunk]:
            total = total + mid[chunk, here, cols].astype(jnp.float32)
        return total

    def wait_ring(chunk):
        for copy in (*pending["near", chunk], *pending["far", chunk]):
            copy.wait_recv()

    def add_cores(chunk):
        pending["core", chunk].wait_recv()
        add_pieces(chunk * CHUNK, CHUNK // 16, core_in, chunk * CHUNK)
        if LINE_FIRST[chunk]:
            pending["line", chunk] = remote(
                part.at[core, line_rows(chunk, 1 - y_hi), :],
                line_in.at[LINE_BUFFER[chunk]],
                to_y,
            )
        else:
            start_ring(chunk)

    def third(chunk):
        if LINE_FIRST[chunk]:
            pending["line", chunk].wait_recv()
            add_pieces(
                chunk * CHUNK + y_hi * 64, 4, line_in.at[LINE_BUFFER[chunk]], 0
            )
            start_ring(chunk)
        else:
            turn_ring(chunk)

    def fourth(chunk):
        if LINE_FIRST[chunk]:
            turn_ring(chunk)
            return
        wait_ring(chunk)
        store_sum(summed.at[chunk], lambda cols: ring_total(chunk, cols))
        other = pl.ds(pl.multiple_of((1 - y_hi) * 16, 16), 16)
        pending["y", chunk] = remote(summed.at[chunk, other, :], y_in.at[chunk], to_y)

    def activate(chunk):
        if LINE_FIRST[chunk]:
            wait_ring(chunk)
        else:
            pending["y", chunk].wait_recv()
        kept = pl.ds(pl.multiple_of(y_hi * 16, 16), 16)

        def total(first, last):
            if LINE_FIRST[chunk]:
                return ring_total(chunk, slice(first, last))
            return summed[chunk, kept, first:last].astype(jnp.float32) + y_in[
                chunk, :, first:last
            ].astype(jnp.float32)

        squares = unpack_sum(total(3 * HALF, PACK), 0)
        inv_rms = lax.rsqrt(squares / D + EPSILON)
        gate_pre = total(0, HALF) * inv_rms
        up_pre = total(HALF, 2 * HALF) * inv_rms
        grad_act = total(2 * HALF, 3 * HALF)
        sigmoid_gate = jax.nn.sigmoid(gate_pre)
        gated = gate_pre * sigmoid_gate
        grad_gate = (
            grad_act * up_pre * sigmoid_gate * (1.0 + gate_pre * (1.0 - sigmoid_gate))
        ).astype(jnp.bfloat16)
        grad_up = (grad_act * gated).astype(jnp.bfloat16)
        inner = jnp.sum(
            grad_gate.astype(jnp.float32) * gate_pre + grad_up.astype(jnp.float32) * up_pre,
            axis=1,
            keepdims=True,
        )
        rows = pl.ds(row_of(chunk, x, y_hi), 16)
        full[core, rows, 0:HALF] = (gated * up_pre).astype(jnp.bfloat16)
        full[core, rows, HALF : 2 * HALF] = grad_gate
        full[core, rows, 2 * HALF : 3 * HALF] = grad_up
        full[core, rows, 3 * HALF :] = pack_sums(inv_rms, inner)
        piece = full.at[core, rows, :]
        pending["y_back", chunk] = [same_place(piece, to_y)]
        pending["x_back", chunk] = [same_place(piece, to_x_up), same_place(piece, to_x_down)]
        pending["x_far", chunk] = []
        if DIRECT_BACK[chunk]:
            pending["x_far", chunk].append(same_place(piece, to_x_far))
        pending["core_back", chunk] = []

    def same_place(piece, device):
        return remote(piece, piece, device)

    def full_rows(chunk, x_at, y_at, rows=16, turn=None):
        cols = pl.ds(0, PACK) if turn is None else pl.ds(*COLUMNS[turn])
        return full.at[core, pl.ds(row_of(chunk, x_at, y_at), rows), cols]

    def to_other_core(chunk, piece):
        pending["core_back", chunk].append(same_place(piece, to_core))

    def wait_all(key, chunk):
        for copy in pending[key, chunk]:
            copy.wait_recv()

    def sixth(chunk):
        if LINE_FIRST[chunk]:
            wait_all("x_back", chunk)
            if not DIRECT_BACK[chunk]:
                pending["x_far", chunk] = (
                    same_place(full_rows(chunk, x_down, y_hi, 16, 0), to_x_up),
                    same_place(full_rows(chunk, x_up, y_hi, 16, 1), to_x_down),
                )
            for x_at in (x_down, x_up):
                pending["y_back", chunk].append(
                    same_place(full_rows(chunk, x_at, y_hi), to_y)
                )
        else:
            wait_all("y_back", chunk)
            piece = full_rows(chunk, x, 1 - y_hi)
            pending["x_back", chunk] += [
                same_place(piece, to_x_up), same_place(piece, to_x_down)
            ]
            if DIRECT_BACK[chunk]:
                pending["x_far", chunk].append(same_place(piece, to_x_far))
            to_other_core(chunk, full_rows(chunk, x, 0, 32))

    def seventh(chunk):
        if LINE_FIRST[chunk]:
            wait_all("x_far", chunk)
            pending["y_back", chunk].append(
                same_place(full_rows(chunk, x_far, y_hi), to_y)
            )
            to_other_core(chunk, full.at[core, line_rows(chunk, y_hi), :])
        else:
            wait_all("x_back", chunk)
            if not DIRECT_BACK[chunk]:
                pending["x_far", chunk] = (
                    same_place(full_rows(chunk, x_down, 0, 32, 0), to_x_up),
                    same_place(full_rows(chunk, x_up, 0, 32, 1), to_x_down),
                )
            to_other_core(chunk, full_rows(chunk, x_down, 0, 32))
            to_other_core(chunk, full_rows(chunk, x_up, 0, 32))

    def eighth(chunk):
        if LINE_FIRST[chunk]:
            wait_all("y_back", chunk)
            to_other_core(chunk, full.at[core, line_rows(chunk, 1 - y_hi), :])
        else:
            wait_all("x_far", chunk)
            to_other_core(chunk, full_rows(chunk, x_far, 0, 32))

    def finish(chunk):
        for copy in pending["core_back", chunk]:
            copy.wait_recv()
        rows = pl.ds(chunk * CHUNK, CHUNK)
        down_sum = dot(full[0, rows, 0:HALF], dw[0], 1, 0) + dot(
            full[1, rows, 0:HALF], dw[1], 1, 0
        )
        back[rows, 0:WIDTH] = down_sum.astype(jnp.bfloat16)
        grad_sum = (
            dot(full[0, rows, HALF : 2 * HALF], gw[0], 1, 1)
            + dot(full[1, rows, HALF : 2 * HALF], gw[1], 1, 1)
            + dot(full[0, rows, 2 * HALF : 3 * HALF], uw[0], 1, 1)
            + dot(full[1, rows, 2 * HALF : 3 * HALF], uw[1], 1, 1)
        )
        back[rows, WIDTH : 2 * WIDTH] = grad_sum.astype(jnp.bfloat16)
        sums = full[0, rows, 3 * HALF :]
        back[rows, 2 * WIDTH :] = pack_sums(
            unpack_sum(sums, 2) + unpack_sum(full[1, rows, 3 * HALF :], 2)
        )
        pending["line_back", chunk] = [
            remote(
                back.at[pl.ds(chunk * CHUNK + place * 64 + OWN, OWN), :],
                line_back.at[chunk, pl.ds(place * OWN, OWN), :],
                to_line,
            )
            for place in range(2)
        ]
        inv_rms = unpack_sum(sums, 0)
        normed[rows, :] = (xt[rows, 0:WIDTH].astype(jnp.float32) * inv_rms * gain_f).astype(
            jnp.bfloat16
        )

    def add_back(chunk):
        wait_all("line_back", chunk)
        for place, offset in enumerate(OFFSETS[chunk]):
            rows = pl.ds(chunk * CHUNK + place * 64, OWN)
            here = pl.ds(place * OWN, OWN)
            plain = slice(0, 2 * WIDTH)
            back[rows, plain] = back[rows, plain] + line_back[chunk, here, plain]
            back[rows, 2 * WIDTH :] = pack_sums(
                unpack_sum(back[rows, 2 * WIDTH :], 0)
                + unpack_sum(line_back[chunk, here, 2 * WIDTH :], 0)
            )
            if offset:
                pending["back", offset] = remote(
                    back.at[rows, :], back_in.at[offset % Z_COUNT], mp_peer(0, offset)
                )

    stages = (
        token_step, products, add_cores, third, fourth, activate, sixth, seventh, eighth, finish,
        add_back,
    )
    for stage, which in ORDER:
        stages[stage](which)

    total = back[own_rows, :].astype(jnp.float32)
    for offset in (1, -1, 2, -2, 3, -3, 4):
        pending["back", offset].wait_recv()
        total = total + back_in[offset % Z_COUNT].astype(jnp.float32)
    inputs_f = xt[own_rows, 0:WIDTH].astype(jnp.float32)
    layer_out[...] = (inputs_f + total[:, 0:WIDTH]).astype(jnp.bfloat16)
    inner_mean = unpack_sum(total[:, 2 * WIDTH :], 0) / D
    inv_rms = unpack_sum(full[0, own_rows, 3 * HALF :], 0)
    grad_scaled = total[:, WIDTH : 2 * WIDTH] * gain_f
    input_grad[...] = (
        xt[own_rows, WIDTH : 2 * WIDTH].astype(jnp.float32)
        + inv_rms * (grad_scaled - inputs_f * inv_rms * inner_mean)
    ).astype(jnp.bfloat16)

    for copy in copies[-SEND_SLOTS:]:
        copy.wait_send()


def weight_kernel(
    sums_out, sums_in, xt, full, normed, gate_m, up_m, down_m,
    layer_out, input_grad, gate_grad, up_grad, down_grad,
    gate_stage, up_stage, down_stage, local,
):
    layer_out[...] = sums_out[...]
    input_grad[...] = sums_in[...]
    marks_d = widen_mask(down_m[...], 8, WIDTH, 0, 0)
    upstream_full = xt[:, WIDTH : 2 * WIDTH]
    stores = []

    def store(src, dst):
        copy = pltpu.make_async_copy(src, dst, local.at[len(stores)])
        copy.start()
        stores.append(copy)

    for half in range(2):
        hidden = pl.ds(half * HALF, HALF)
        grads = dot(full[half, :, 0:HALF], upstream_full, 0, 0)
        for block in range(HALF // BLOCK):
            rows = slice(block * BLOCK, (block + 1) * BLOCK)
            mark = half * (HALF // BLOCK) + block
            down_stage[half, rows, :] = (
                grads[rows, :] * marks_d[mark : mark + 1, :]
            ).astype(jnp.bfloat16)
        store(down_stage.at[half], down_grad.at[hidden, :])
        for which, stage, given, target in (
            (0, gate_stage, gate_m, gate_grad), (1, up_stage, up_m, up_grad)
        ):
            first = (1 + which) * HALF
            marks = widen_mask(given[...], 28, HALF, half * HALF)
            grads = dot(normed[...], full[half, :, first : first + HALF], 0, 0)
            for block in range(WIDTH // BLOCK):
                rows = slice(block * BLOCK, (block + 1) * BLOCK)
                stage[half, rows, :] = (grads[rows, :] * marks[block : block + 1, :]).astype(
                    jnp.bfloat16
                )
            store(stage.at[half], target.at[:, hidden])
    for copy in stores:
        copy.wait()


def on_device(
    tokens, upstream, norm_gain, gate_weight, up_weight, down_weight, gate_mask, up_mask, down_mask
):
    in_vmem = pl.BlockSpec(memory_space=pltpu.VMEM)
    anywhere = pl.BlockSpec(memory_space=pl.ANY)
    bf16 = jnp.bfloat16
    down_marks = down_mask.T
    sums_out, sums_in, xt, full, normed = pl.pallas_call(
        kernel,
        out_shape=(
            pltpu.VMEM((OWN, WIDTH), bf16),
            pltpu.VMEM((OWN, WIDTH), bf16),
            pltpu.VMEM((TOKENS, 2 * WIDTH), bf16),
            pltpu.VMEM((2, TOKENS, PACK), bf16),
            pltpu.VMEM((TOKENS, WIDTH), bf16),
        ),
        in_specs=[anywhere, anywhere, in_vmem] + [anywhere] * 3 + [in_vmem] * 3,
        out_specs=[in_vmem] * 5,
        scratch_shapes=[
            pltpu.VMEM((2, WIDTH, HALF), bf16),
            pltpu.VMEM((2, WIDTH, HALF), bf16),
            pltpu.VMEM((2, HALF, WIDTH), bf16),
            pltpu.VMEM((2, 8, HALF), jnp.float32),
            pltpu.VMEM((2, 8, HALF), jnp.float32),
            pltpu.VMEM((28, WIDTH), jnp.float32),
            pltpu.VMEM((2, TOKENS, PACK), bf16),
            pltpu.VMEM((TOKENS, PACK), bf16),
            pltpu.VMEM((CHUNKS, 32, PACK), bf16),
            pltpu.VMEM((CHUNKS, 32, PACK), bf16),
            pltpu.VMEM((CHUNKS, 32, PACK), bf16),
            pltpu.VMEM((CHUNKS, 32, PACK), bf16),
            pltpu.VMEM((CHUNKS, 16, PACK), bf16),
            pltpu.VMEM((1, 64, PACK), bf16),
            pltpu.VMEM((TOKENS, BACK), bf16),
            pltpu.VMEM((CHUNKS, 64, BACK), bf16),
            pltpu.VMEM((Z_COUNT, OWN, BACK), bf16),
            pltpu.SemaphoreType.DMA((SEND_SLOTS,)),
            pltpu.SemaphoreType.DMA((COPY_SLOTS,)),
            pltpu.SemaphoreType.DMA((LOCAL_SLOTS,)),
        ],
        compiler_params=pltpu.CompilerParams(
            collective_id=0, has_side_effects=True, vmem_limit_bytes=55 * 1024 * 1024
        ),
    )(
        tokens, upstream, norm_gain, gate_weight, up_weight, down_weight,
        gate_mask, up_mask, down_marks,
    )
    return pl.pallas_call(
        weight_kernel,
        out_shape=(
            jax.ShapeDtypeStruct((OWN, WIDTH), bf16),
            jax.ShapeDtypeStruct((OWN, WIDTH), bf16),
            jax.ShapeDtypeStruct((WIDTH, 2 * HALF), bf16),
            jax.ShapeDtypeStruct((WIDTH, 2 * HALF), bf16),
            jax.ShapeDtypeStruct((2 * HALF, WIDTH), bf16),
        ),
        in_specs=[in_vmem] * 8,
        out_specs=[in_vmem, in_vmem, anywhere, anywhere, anywhere],
        scratch_shapes=[
            pltpu.VMEM((2, WIDTH, HALF), bf16),
            pltpu.VMEM((2, WIDTH, HALF), bf16),
            pltpu.VMEM((2, HALF, WIDTH), bf16),
            pltpu.SemaphoreType.DMA((6,)),
        ],
        compiler_params=pltpu.CompilerParams(vmem_limit_bytes=24 * 1024 * 1024),
    )(sums_out, sums_in, xt, full, normed, gate_mask, up_mask, down_marks)


def solution(mesh):
    in_specs = (
        P("mp", "section"),
        P("mp", "section"),
        P("section"),
        P("section", "mp"),
        P("section", "mp"),
        P("mp", "section"),
        P("section", "mp"),
        P("section", "mp"),
        P("mp", "section"),
    )
    out_specs = (
        P("mp", "section"),
        P("mp", "section"),
        P("section", "mp"),
        P("section", "mp"),
        P("mp", "section"),
    )
    return jax.shard_map(
        on_device, mesh=mesh, in_specs=in_specs, out_specs=out_specs, check_vma=False
    )
```
